256 devices in a mesh: ctx: 8 (over z), tp: 32 (over y, x, core).
Axes of the slice: x: 4, y: 4, z: 8, core: 2. Of those that a mesh axis runs over, the one named last changes fastest.
Arguments:
- tokens: bfloat16 [1024, 8192], P('ctx', 'tp'), may hold values from -6 to 6
- inner_weight: bfloat16 [8192, 8192], P(None, 'tp'), may hold values from -0.0625 to 0.0625
- gate_weight: bfloat16 [8192, 8192], P(None, 'tp'), may hold values from -0.0625 to 0.0625
- conv_weight: float32 [4, 8192], P(None, 'tp'), may hold values from -3 to 3
- conv_bias: float32 [8192], P('tp'), may hold values from -3 to 3
- proj_weight: bfloat16 [8192, 544], P('tp'), may hold values from -0.0625 to 0.0625
- step_weight: bfloat16 [512, 8192], P(None, 'tp'), may hold values from -0.25 to 0.25
- step_bias: float32 [8192], P('tp'), may hold values from -4 to -0.5
- decay_rate: float32 [8192, 16], P('tp'), may hold values from 1e-05 to 2
- skip_gain: float32 [8192], P('tp'), may hold values from -1 to 2
- out_weight: bfloat16 [8192, 8192], P('tp'), may hold values from -0.125 to 0.125
- carried_state: float32 [8192, 16], P('tp'), may hold values from -6 to 6
Outputs:
- mixed: bfloat16 [1024, 8192], P('ctx', 'tp')
- boundary_states: float32 [8, 8192, 16], P('ctx', 'tp')
The draws below stay inside these ranges and needn't reach their ends.
All inputs are finite; a program needn't handle non-finite values.
Results may differ from the reference program's by a relative error of at most 0.025.
Values may be sent and summed in bfloat16 or wider, within the bound.
A program may use at most 64 MiB of HBM per device.

```python
import jax
import jax.numpy as jnp
from jax import lax

D = 8192
STATE = 16
CONV = 4
DT_RANK = 512
INNER = 8192
L_DEV = 128
TOKENS = 1024
N_CTX = 8
N_TP = 32


def quick_channels(key):
    return jax.random.uniform(jax.random.fold_in(key, 11), (INNER,), jnp.float32) < 0.4


def draw_step_bias(key, part):
    quick = quick_channels(key)
    spread = jax.random.uniform(jax.random.fold_in(key, 12), (INNER,), jnp.float32)
    quick_value = -1.5 + spread
    slow_value = -4.0 + 2.5 * spread
    return jnp.where(quick, quick_value, slow_value).astype(jnp.float32)


def draw_decay_rate(key, part):
    quick = quick_channels(key)[:, None]
    spread = jax.random.uniform(jax.random.fold_in(key, 13), (INNER, STATE), jnp.float32)
    low_log = jnp.log(jnp.float32(1e-05))
    high_log = jnp.log(jnp.float32(2.0))
    slow_value = jnp.exp(low_log + spread * (high_log - low_log))
    quick_value = jnp.exp(jnp.log(jnp.float32(0.5)) + spread * jnp.log(jnp.float32(4.0)))
    return jnp.clip(jnp.where(quick, quick_value, slow_value), 1e-05, 2.0).astype(jnp.float32)


def with_spikes(values, rng, source, target, parts, factor):
    def block_of(position):
        return (jnp.arange(values.shape[position]) // (values.shape[position] // parts)).reshape((-1,) + (1,) * (values.ndim - 1 - position))

    first = jax.random.permutation(rng, parts)[block_of(target)]
    far = (block_of(target) + parts // 2) % parts
    return jnp.where((block_of(source) == first) | (block_of(source) == far), factor * values, values)


def shard_levels(stream_key, shape, cuts, least, top_value):
    level = 1.0
    for position, parts in cuts:
        draws = jax.random.uniform(jax.random.fold_in(jax.random.fold_in(stream_key, 6), position), (parts,), jnp.float32, least / len(cuts), top_value / len(cuts))
        level = level * jnp.repeat(jnp.exp(draws), shape[position] // parts).reshape((-1,) + (1,) * (len(shape) - 1 - position))
    return level


def scatter_about(key, shape, scale, bound, shards=(), held_as=jnp.bfloat16):
    level = shard_levels(key, shape, shards, -0.22, 0.18) if shards else 1.0
    entries = jax.random.normal(key, shape, jnp.float32) * scale * level
    return jnp.minimum(jnp.maximum(entries, -bound), bound).astype(held_as)


def gaussian_with(rng, extent, width, most, shards, heavy, kind=jnp.bfloat16):
    result = width * jax.random.normal(rng, extent, jnp.float32)
    if shards:
        result = result * shard_levels(rng, extent, shards, -0.22, 0.18)
    return jnp.clip(with_spikes(result, jax.random.fold_in(rng, 3), *heavy), -most, most).astype(kind)


def setup_inputs(seed: int = 0) -> dict:
    arg_keys = jax.random.split(jax.random.key(seed), 13)
    tokens = scatter_about(arg_keys[0], (TOKENS, D), 1.0, 6.0, ((0, 8), (1, 32)))
    inner_weight = scatter_about(arg_keys[1], (D, INNER), D ** -0.5, 0.0625, ((1, 32),))
    gate_weight = scatter_about(arg_keys[2], (D, INNER), D ** -0.5, 0.0625, ((1, 32),))
    conv_weight = scatter_about(arg_keys[3], (CONV, INNER), CONV ** -0.5, 3.0, ((1, 32),), jnp.float32)
    conv_bias = scatter_about(arg_keys[4], (INNER,), 0.5, 3.0, ((0, 32),), jnp.float32)
    proj_weight = scatter_about(arg_keys[5], (INNER, DT_RANK + 2 * STATE), INNER ** -0.5, 0.0625, ((0, 32),))
    step_weight = scatter_about(arg_keys[6], (DT_RANK, INNER), DT_RANK ** -0.5, 0.25, ((1, 32),))
    step_bias = draw_step_bias(jax.random.fold_in(arg_keys[12], 71), 0)
    decay_rate = draw_decay_rate(jax.random.fold_in(arg_keys[12], 71), 0)
    skip_gain = jnp.clip(-1.0 + 3.0 * jax.random.uniform(arg_keys[9], (INNER,), jnp.float32) ** shard_levels(arg_keys[9], (INNER,), ((0, 32),), -0.2, 0.2), -1.0, 2.0)
    out_weight = gaussian_with(arg_keys[10], (INNER, D), INNER ** -0.5, 0.125, ((0, 32),), (0, 1, 32, 2.75))
    carried_state = scatter_about(arg_keys[11], (INNER, STATE), 1.0, 6.0, ((0, 32),), jnp.float32)
    return {"tokens": tokens, "inner_weight": inner_weight, "gate_weight": gate_weight, "conv_weight": conv_weight, "conv_bias": conv_bias, "proj_weight": proj_weight, "step_weight": step_weight, "step_bias": step_bias, "decay_rate": decay_rate, "skip_gain": skip_gain, "out_weight": out_weight, "carried_state": carried_state}


def conv_inner(inner_x, conv_weight, conv_bias, count):
    kernel = conv_weight.shape[0]
    leading_rows = jnp.zeros((kernel - 1, inner_x.shape[1]), jnp.float32)
    padded = jnp.concatenate([leading_rows, inner_x.astype(jnp.float32)], axis=0)
    summed = jnp.broadcast_to(conv_bias[None, :], (count, conv_bias.shape[0]))
    for offset in range(kernel):
        summed = summed + conv_weight[offset][None, :] * padded[offset:offset + count]
    return jax.nn.silu(summed).astype(jnp.bfloat16)


def reference(tokens, inner_weight, gate_weight, conv_weight, conv_bias, proj_weight, step_weight, step_bias, decay_rate, skip_gain, out_weight, carried_state):
    inner_x = jnp.dot(tokens, inner_weight, preferred_element_type=jnp.float32).astype(jnp.bfloat16)
    gate = jnp.dot(tokens, gate_weight, preferred_element_type=jnp.float32).astype(jnp.bfloat16)
    conv_x = conv_inner(inner_x, conv_weight, conv_bias, TOKENS)
    proj = jnp.dot(conv_x, proj_weight, preferred_element_type=jnp.float32)
    low = proj[:, :DT_RANK].astype(jnp.bfloat16)
    step = jax.nn.softplus(jnp.dot(low, step_weight, preferred_element_type=jnp.float32) + step_bias[None, :])
    b_in = proj[:, DT_RANK:DT_RANK + STATE]
    c_out = proj[:, DT_RANK + STATE:]
    conv_float = conv_x.astype(jnp.float32)

    def token_step(hidden, inputs):
        step_row, b_row, c_row, x_row = inputs
        hidden = jnp.exp(-step_row[:, None] * decay_rate) * hidden + (step_row * x_row)[:, None] * b_row[None, :]
        return hidden, jnp.sum(hidden * c_row[None, :], axis=1)

    def shard_step(hidden, inputs):
        hidden, readout = lax.scan(token_step, hidden, inputs)
        return hidden, (readout, hidden)

    shaped = tuple(v.reshape((N_CTX, L_DEV) + v.shape[1:]) for v in (step, b_in, c_out, conv_float))
    final_state, (readout, boundary_states) = lax.scan(shard_step, carried_state.astype(jnp.float32), shaped)
    readout = readout.reshape(TOKENS, INNER)
    gated = ((readout + skip_gain[None, :] * conv_float) * jax.nn.silu(gate.astype(jnp.float32))).astype(jnp.bfloat16)
    block = INNER // N_TP
    gated_blocks = jnp.transpose(gated.reshape(TOKENS, N_TP, block), (1, 0, 2))
    weight_blocks = out_weight.reshape(N_TP, block, D)

    def add_block(total, pair):
        gated_part, weight_part = pair
        partial_value = jnp.dot(gated_part, weight_part, preferred_element_type=jnp.float32).astype(jnp.bfloat16)
        return total + partial_value.astype(jnp.float32), None

    total, unused = lax.scan(add_block, jnp.zeros((TOKENS, D), jnp.float32), (gated_blocks, weight_blocks))
    mixed = total.astype(jnp.bfloat16)
    return mixed, boundary_states
```

```python
import functools

import jax
import jax.numpy as jnp
from jax import lax
from jax.experimental import pallas as pl
from jax.experimental.pallas import tpu as pltpu
from jax.sharding import PartitionSpec as P

STATE = 16
DT_RANK = 512
MESH = pl.DeviceIdType.MESH
BF16 = jnp.bfloat16
F32 = jnp.float32


def dot(a, b):
    return jnp.dot(a, b, preferred_element_type=F32)


def dot_t(a, b):
    return lax.dot_general(a, b, (((1,), (1,)), ((), ())), preferred_element_type=F32)


def silu(v):
    return v * jax.nn.sigmoid(v)


def plane_sides(n_tp):
    chips = n_tp // 2
    side = 1
    while side * side < chips:
        side *= 2
    return chips // side, side


def kernel(
    n_ctx, n_tp, tokens_hbm, iw_hbm, gw_hbm, cw_hbm, cb_hbm, pw_hbm, sw_hbm, sb_hbm, dr_hbm, sg_hbm, ow_hbm, cs_hbm,
    mixed, boundary,
    x_buf, iw, gw, ow, pw, sw, cw, cb, sb, sg, dr, cs, acc, gate, pad, tail_in,
    p_send, p_recv, p_more, p_res, step_ref, drive_ref, conv_ref, h_buf, b_chunk, c_chunk, state_out, state_in, q_buf, y_buf,
    part, sib_part, mine, s1_send, s1_a, s1_b, s2_send, s2_a, s2_b,
    load_sem, own_send, own_recv, sib_send, sib_recv, tail_sem, red_sem, more_sem, res_sem, state_send, state_recv,
    rs_sib_send, rs_sib_recv, s1_send_sem, s1_a_sem, s1_b_sem, s2_send_sem, s2_a_sem, s2_b_sem,
):
    ny, nx = plane_sides(n_tp)
    chips = ny * nx
    rows, width = tokens_hbm.shape
    half = rows // 2
    s, me = lax.axis_index("ctx"), lax.axis_index("tp")
    core, chip = lax.rem(me, 2), me // 2
    cx, cy = lax.rem(chip, nx), chip // nx

    def chip_at(dx, dy):
        return lax.rem(cy + dy + ny, ny) * nx + lax.rem(cx + dx + nx, nx)

    def tp_at(dx, dy, other=False):
        return chip_at(dx, dy) * 2 + ((1 - core) if other else core)

    def remote(src, dst, send, recv, to, ctx=None):
        return pltpu.make_async_remote_copy(
            src_ref=src, dst_ref=dst, send_sem=send, recv_sem=recv,
            device_id=(s if ctx is None else ctx, to), device_id_type=MESH,
        )

    def await_recv(ref, sem):
        remote(ref, ref, sem, sem, me).wait_recv()

    def await_send(ref, sem):
        remote(ref, ref, sem, sem, me).wait_send()

    loads = []
    for k, (src, dst) in enumerate(
        [(tokens_hbm, x_buf.at[me]), (iw_hbm, iw), (gw_hbm, gw), (pw_hbm, pw), (sw_hbm, sw), (cw_hbm, cw), (cb_hbm, cb),
         (sb_hbm, sb), (sg_hbm, sg), (dr_hbm, dr), (cs_hbm, cs), (ow_hbm, ow)]
    ):
        loads.append(pltpu.make_async_copy(src, dst, load_sem.at[k]))
        loads[-1].start()

    barrier = pltpu.get_barrier_semaphore()
    for i in range(1, n_tp):
        pl.semaphore_signal(barrier, inc=1, device_id=(s, lax.rem(me + i, n_tp)), device_id_type=MESH)
    for i in range(1, n_ctx):
        pl.semaphore_signal(barrier, inc=1, device_id=(lax.rem(s + i, n_ctx), me), device_id_type=MESH)
    loads[0].wait()
    pl.semaphore_wait(barrier, n_tp + n_ctx - 2)

    top, bottom = pl.ds(0, half), pl.ds(half, half)
    far_first_x = sorted(range(1, nx), key=lambda d: -min(d, nx - d))
    far_first_y = sorted(range(1, ny), key=lambda d: -min(d, ny - d))
    near_x, near_y = far_first_x[::-1], far_first_y[::-1]

    def send_piece(piece, h, dx, dy, rx, ry):
        view = x_buf.at[piece, bottom if h else top]
        remote(view, view, own_send, own_recv.at[rx * ny + ry, h], tp_at(dx, dy)).start()

    def await_piece(rx, ry, h):
        view = x_buf.at[tp_at(-rx, -ry), bottom if h else top]
        await_recv(view, own_recv.at[rx * ny + ry, h])

    def to_sibling(rx, ry):
        view = x_buf.at[tp_at(-rx, -ry)]
        remote(view, view, sib_send, sib_recv.at[rx * ny + ry], tp_at(0, 0, True)).start()

    def from_sibling(rx, ry):
        await_recv(x_buf.at[tp_at(-rx, -ry, True)], sib_recv.at[rx * ny + ry])

    for k in range(max(nx, ny) - 1):
        if k < nx - 1:
            send_piece(me, 0, far_first_x[k], 0, far_first_x[k], 0)
        if k < ny - 1:
            send_piece(me, 1, 0, far_first_y[k], 0, far_first_y[k])
    to_sibling(0, 0)
    for k in range(max(nx, ny) - 1):
        if k < ny - 1:
            send_piece(me, 0, 0, far_first_y[k], 0, far_first_y[k])
        if k < nx - 1:
            send_piece(me, 1, far_first_x[k], 0, far_first_x[k], 0)

    def times(piece, weight):
        first = pl.multiple_of(piece * width, width)
        return dot(x_buf[piece], weight[pl.ds(first, width), :])

    def add_inner(pieces, fresh=False):
        total = sum(times(p, iw) for p in pieces)
        acc[...] = total if fresh else acc[...] + total

    for load in loads[1:]:
        load.wait()
    decay, carried = dr[...], cs[...]
    from_sibling(0, 0)
    add_inner([tp_at(0, 0), tp_at(0, 0, True)], fresh=True)

    waiting = []
    for k in range(max(nx, ny) - 1):
        group = []
        if k < nx - 1:
            d = near_x[k]
            await_piece(d, 0, 0)
            for e in far_first_y:
                send_piece(tp_at(-d, 0), 0, 0, e, d, e)
            group.append((d, 0))
        if k < ny - 1:
            d = near_y[k]
            await_piece(0, d, 1)
            for e in far_first_x:
                send_piece(tp_at(0, -d), 1, e, 0, e, d)
            group.append((0, d))
        for rx, ry in group:
            await_piece(rx, ry, 1 if ry == 0 else 0)
            to_sibling(rx, ry)
        for rx, ry in waiting:
            from_sibling(rx, ry)
        add_inner([tp_at(-a, -b) for a, b in group] + [tp_at(-a, -b, True) for a, b in waiting])
        waiting = group
    rest = sorted(
        [(a, b) for a in range(1, nx) for b in range(1, ny)],
        key=lambda r: max(near_x.index(r[0]), near_y.index(r[1])) * 10 + near_x.index(r[0]) + near_y.index(r[1]),
    )
    for k in range(0, len(rest), 3):
        group = rest[k : k + 3]
        for rx, ry in group:
            await_piece(rx, ry, 0)
            await_piece(rx, ry, 1)
            to_sibling(rx, ry)
        for rx, ry in waiting:
            from_sibling(rx, ry)
        add_inner([tp_at(-a, -b) for a, b in group] + [tp_at(-a, -b, True) for a, b in waiting])
        waiting = group
    for rx, ry in waiting:
        from_sibling(rx, ry)
    add_inner([tp_at(-a, -b, True) for a, b in waiting])

    pad[8:, :] = acc[...].astype(BF16).astype(F32)
    tail = pad.at[pl.ds(rows, 8)]
    first_shard = s == 0

    @pl.when(s < n_ctx - 1)
    def _():
        remote(tail, tail_in, tail_sem.at[0], tail_sem.at[1], me, ctx=lax.rem(s + 1, n_ctx)).start()

    gate[...] = sum(times(p, gw) for p in range(n_tp)).astype(BF16).astype(F32)

    @pl.when(first_shard)
    def _():
        tail_in[...] = jnp.zeros_like(tail_in)

    @pl.when(s > 0)
    def _():
        await_recv(tail_in, tail_sem.at[1])

    pad[0:8, :] = tail_in[...]
    taps = cw.shape[0]
    summed = cb[...] + cw[0:1, :] * pad[9 - taps : 9 - taps + rows, :]
    for k in range(1, taps):
        summed = summed + cw[k : k + 1, :] * pad[9 - taps + k : 9 - taps + k + rows, :]
    conv_low = silu(summed).astype(BF16)
    conv_ref[...] = conv_low.astype(F32)

    each = p_send.shape[1]
    proj = dot_t(conv_low, pw[:DT_RANK, :]).astype(BF16)
    across = DT_RANK // 128
    for block in range(n_tp * each):
        r, c = block // across, block % across
        p_send[block // each, block % each] = proj[r * 16 : r * 16 + 16, c * 128 : c * 128 + 128]
    bc = dot_t(pw[DT_RANK:, :], conv_low).astype(BF16)
    p_more[0, me] = bc[:STATE]
    p_more[1, me] = bc[STATE:]
    owners = (0, n_tp // 2)
    for i in range(1, n_tp):
        to = lax.rem(me + i, n_tp)
        remote(p_send.at[to], p_recv.at[me], red_sem.at[0], red_sem.at[1], to).start()
    for which, owner in enumerate(owners):
        mine_too = p_more.at[which, me]

        @pl.when(me != owner)
        def _():
            remote(mine_too, mine_too, more_sem.at[which, 0], more_sem.at[which, 1], owner).start()

    p_recv[me] = p_send[me]
    await_recv(p_recv.at[pl.ds(0, n_tp - 1)], red_sem.at[1])
    total = p_recv[0].astype(F32)
    for i in range(1, n_tp):
        total = total + p_recv[i].astype(F32)
    p_res[pl.ds(me * each, each)] = total.astype(BF16)
    result = p_res.at[pl.ds(me * each, each)]
    for i in range(1, n_tp):
        remote(result, result, res_sem.at[0], res_sem.at[1], lax.rem(me + i, n_tp)).start()
    blocks = n_tp * each
    for which, owner in enumerate(owners):
        place = p_res.at[pl.ds(blocks + which, 1)]

        @pl.when(me == owner)
        def _():
            await_recv(p_more.at[which, pl.ds(0, n_tp - 1)], more_sem.at[which, 1])
            total = p_more[which, 0].astype(F32)
            for i in range(1, n_tp):
                total = total + p_more[which, i].astype(F32)
            p_res[blocks + which] = total.astype(BF16)
            for i in range(1, n_tp):
                remote(place, place, more_sem.at[which, 2], more_sem.at[which, 3], lax.rem(me + i, n_tp)).start()

    await_recv(p_res.at[pl.ds(0, (n_tp - 1) * each)], res_sem.at[1])
    low = jnp.concatenate(
        [jnp.concatenate([p_res[r * across + c] for c in range(across)], axis=1) for r in range(rows // 16)], axis=0
    )
    step = jax.nn.softplus(dot(low, sw[...]) + sb[...])
    step_ref[...] = step
    drive_ref[...] = step * conv_ref[...]
    later = lax.broadcasted_iota(jnp.int32, (rows, rows), 0)
    earlier = lax.broadcasted_iota(jnp.int32, (rows, rows), 1)
    below = (earlier <= later).astype(F32)
    so_far = jnp.dot(below, step, preferred_element_type=F32, precision=lax.Precision.HIGHEST)

    for which, owner in enumerate(owners):

        @pl.when(me != owner)
        def _():
            await_recv(p_res.at[pl.ds(blocks + which, 1)], more_sem.at[which, 3])

    b_t, c_t = p_res[blocks].astype(F32), p_res[blocks + 1].astype(F32)
    run = 16
    for k in range(rows // run):
        turn = (rows - k * run) % rows
        b_chunk[k] = pltpu.roll(b_t, turn, 1) if turn else b_t
        c_chunk[k] = pltpu.roll(c_t, turn, 1) if turn else c_t

    def scan_chunk(k, h):
        first = pl.multiple_of(k * run, run)
        steps, drives, bs = step_ref[pl.ds(first, run), :], drive_ref[pl.ds(first, run), :], b_chunk[k]
        for i in range(run):
            h = jnp.exp(-steps[i : i + 1, :] * decay) * h + drives[i : i + 1, :] * bs[:, i : i + 1]
            h_buf[first + i] = h
        return h

    end = lax.fori_loop(0, rows // run, scan_chunk, jnp.zeros((STATE, width), F32))

    state_out[0:STATE, :] = end
    state_out[STATE:, :] = jnp.broadcast_to(so_far[rows - 1 :, :], (8, width))
    for d in range(1, n_ctx):

        @pl.when(s + d < n_ctx)
        def _():
            remote(
                state_out, state_in.at[n_ctx - 1 - d], state_send.at[d], state_recv.at[d], me, ctx=lax.rem(s + d, n_ctx)
            ).start()

    def read_chunk(k, carry):
        first = pl.multiple_of(k * run, run)
        c_now = c_chunk[k]
        lines = []
        for i in range(run):
            lines.append(jnp.sum(h_buf[first + i] * c_now[:, i : i + 1], axis=0, keepdims=True))
        y_buf[pl.ds(first, run), :] = jnp.concatenate(lines, axis=0)
        return carry

    lax.fori_loop(0, rows // run, read_chunk, 0)
    c_rows = jnp.transpose(c_t)
    for n in range(STATE):
        q_buf[n] = c_rows[:, n : n + 1] * jnp.exp(-so_far * decay[n : n + 1, :])
    y_buf[...] = y_buf[...] + sg[...] * conv_ref[...]
    gate[...] = silu(gate[...])

    for d in range(1, n_ctx):

        @pl.when(s >= d)
        def _():
            await_recv(state_in.at[n_ctx - 1 - d], state_recv.at[d])

    def enter(i, e):
        got = state_in[i]
        return jnp.exp(-decay * got[STATE : STATE + 1, :]) * e + got[:STATE, :]

    entering = lax.fori_loop(n_ctx - 1 - s, n_ctx - 1, enter, carried)
    boundary[...] = jnp.exp(-decay * state_out[STATE : STATE + 1, :]) * entering + end

    readout = y_buf[...]
    for n in range(STATE):
        readout = readout + q_buf[n] * entering[n : n + 1, :]
    gated = (readout * gate[...]).astype(BF16)

    def out_piece(piece):
        first = pl.multiple_of(piece * width, width)
        return dot(gated, ow[:, pl.ds(first, width)])

    def combine(ex, ey):
        r = ex * ny + ey
        await_recv(sib_part.at[r], rs_sib_recv.at[r])
        total = mine[r] + sib_part[r].astype(F32)
        mine[r] = total
        s1_send[r] = total.astype(BF16)
        if ey:
            remote(s1_send.at[r, top], s1_a.at[ey, ex], s1_send_sem, s1_a_sem.at[ey, ex], tp_at(0, ey)).start()
        if ex:
            remote(s1_send.at[r, bottom], s1_b.at[ex, ey], s1_send_sem, s1_b_sem.at[ex, ey], tp_at(ex, 0)).start()

    order = [(a, b) for a in far_first_x for b in far_first_y]
    order += [(0, b) for b in far_first_y] + [(a, 0) for a in far_first_x] + [(0, 0)]
    lag = 2
    for k, (ex, ey) in enumerate(order):
        r = ex * ny + ey
        part[r] = out_piece(tp_at(ex, ey, True)).astype(BF16)
        remote(part.at[r], sib_part.at[r], rs_sib_send, rs_sib_recv.at[r], tp_at(0, 0, True)).start()
        mine[r] = out_piece(tp_at(ex, ey))
        if k >= lag:
            combine(*order[k - lag])
    for k in range(max(0, len(order) - lag), len(order)):
        combine(*order[k])

    def second_a(ex):
        total = mine[ex * ny, top, :]
        for e in range(1, ny):
            await_recv(s1_a.at[e, ex], s1_a_sem.at[e, ex])
            total = total + s1_a[e, ex].astype(F32)
        return total

    def second_b(ey):
        total = mine[ey, bottom, :]
        for e in range(1, nx):
            await_recv(s1_b.at[e, ey], s1_b_sem.at[e, ey])
            total = total + s1_b[e, ey].astype(F32)
        return total

    for k in range(max(nx, ny) - 1):
        if k < nx - 1:
            d = far_first_x[k]
            s2_send[0, d] = second_a(d).astype(BF16)
            remote(s2_send.at[0, d], s2_a.at[d], s2_send_sem.at[0, d], s2_a_sem.at[d], tp_at(d, 0)).start()
        if k < ny - 1:
            d = far_first_y[k]
            s2_send[1, d] = second_b(d).astype(BF16)
            remote(s2_send.at[1, d], s2_b.at[d], s2_send_sem.at[1, d], s2_b_sem.at[d], tp_at(0, d)).start()
    upper, lower = second_a(0), second_b(0)
    for d in near_x:
        await_recv(s2_a.at[d], s2_a_sem.at[d])
        upper = upper + s2_a[d].astype(F32)
    mixed[0:half, :] = upper.astype(BF16)
    for d in near_y:
        await_recv(s2_b.at[d], s2_b_sem.at[d])
        lower = lower + s2_b[d].astype(F32)
    mixed[half:, :] = lower.astype(BF16)

    await_send(x_buf.at[pl.ds(0, chips - 1)], own_send)
    await_send(x_buf.at[pl.ds(0, chips)], sib_send)

    @pl.when(s < n_ctx - 1)
    def _():
        await_send(tail, tail_sem.at[0])

    await_send(p_recv.at[pl.ds(0, n_tp - 1)], red_sem.at[0])
    await_send(p_res.at[pl.ds(0, (n_tp - 1) * each)], res_sem.at[0])
    for which, owner in enumerate(owners):

        @pl.when(me != owner)
        def _():
            await_send(p_more.at[which, 0], more_sem.at[which, 0])

        @pl.when(me == owner)
        def _():
            await_send(p_more.at[which, pl.ds(0, n_tp - 1)], more_sem.at[which, 2])

    for d in range(1, n_ctx):

        @pl.when(s + d < n_ctx)
        def _():
            await_send(state_out, state_send.at[d])

    await_send(sib_part, rs_sib_send)
    for a in range(nx):
        for b in range(ny):
            if b:
                await_send(s1_send.at[0, top], s1_send_sem)
            if a:
                await_send(s1_send.at[0, top], s1_send_sem)
    for d in range(1, nx):
        await_send(s2_send.at[0, d], s2_send_sem.at[0, d])
    for d in range(1, ny):
        await_send(s2_send.at[1, d], s2_send_sem.at[1, d])


def on_device(
    n_ctx, n_tp, tokens, inner_weight, gate_weight, conv_weight, conv_bias, proj_weight, step_weight, step_bias, decay_rate,
    skip_gain, out_weight, carried_state,
):
    rows, width = tokens.shape
    depth = inner_weight.shape[0]
    ny, nx = plane_sides(n_tp)
    chips = ny * nx
    half = rows // 2
    each = (rows // 16) * (DT_RANK // 128) // n_tp
    vmem, dma = pltpu.VMEM, pltpu.SemaphoreType.DMA
    args = (
        tokens, inner_weight, gate_weight, conv_weight, conv_bias[None, :], jnp.transpose(proj_weight), step_weight,
        step_bias[None, :], jnp.transpose(decay_rate), skip_gain[None, :], out_weight, jnp.transpose(carried_state),
    )
    held = (inner_weight, gate_weight, out_weight, args[5], step_weight, conv_weight)
    mixed, boundary = pl.pallas_call(
        functools.partial(kernel, n_ctx, n_tp),
        out_shape=(
            jax.ShapeDtypeStruct((rows, width), BF16),
            jax.ShapeDtypeStruct((STATE, width), F32),
        ),
        in_specs=[pl.BlockSpec(memory_space=pl.ANY)] * len(args),
        out_specs=[pl.BlockSpec(memory_space=pltpu.VMEM)] * 2,
        scratch_shapes=[
            vmem((n_tp, rows, width), BF16),
            *[vmem(a.shape, a.dtype) for a in held],
            *[vmem((1, width), F32)] * 3,
            *[vmem((STATE, width), F32)] * 2,
            *[vmem((rows, width), F32)] * 2,
            vmem((rows + 8, width), F32),
            vmem((8, width), F32),
            vmem((n_tp, each, 16, 128), BF16),
            vmem((n_tp, each, 16, 128), BF16),
            vmem((2, n_tp, STATE, 128), BF16),
            vmem((n_tp * each + 2, 16, 128), BF16),
            *[vmem((rows, width), F32)] * 3,
            vmem((rows, STATE, width), F32),
            *[vmem((rows // 16, STATE, rows), F32)] * 2,
            vmem((STATE + 8, width), F32),
            vmem((n_ctx, STATE + 8, width), F32),
            vmem((STATE, rows, width), F32),
            vmem((rows, width), F32),
            *[vmem((chips, rows, width), BF16)] * 2,
            vmem((chips, rows, width), F32),
            vmem((chips, rows, width), BF16),
            vmem((ny, nx, half, width), BF16),
            vmem((nx, ny, half, width), BF16),
            vmem((2, max(nx, ny), half, width), BF16),
            vmem((nx, half, width), BF16),
            vmem((ny, half, width), BF16),
            dma((len(args),)),
            dma,
            dma((chips, 2)),
            dma,
            dma((chips,)),
            dma((2,)),
            dma((2,)),
            dma((2, 4)),
            dma((2,)),
            dma((n_ctx,)),
            dma((n_ctx,)),
            dma,
            dma((chips,)),
            dma,
            dma((ny, nx)),
            dma((nx, ny)),
            dma((2, max(nx, ny))),
            dma((nx,)),
            dma((ny,)),
        ],
        compiler_params=pltpu.CompilerParams(collective_id=0, has_side_effects=True, vmem_limit_bytes=56 << 20),
        cost_estimate=pl.CostEstimate(
            flops=2 * rows * width * (3 * depth + 544 + 512), bytes_accessed=3 * depth * width * 2, transcendentals=0
        ),
        name="layer",
    )(*args)
    return mixed, jnp.transpose(boundary)[None]


def solution(mesh):
    in_specs = (
        P("ctx", "tp"), P(None, "tp"), P(None, "tp"), P(None, "tp"), P("tp"), P("tp", None), P(None, "tp"), P("tp"),
        P("tp", None), P("tp"), P("tp", None), P("tp", None),
    )
    out_specs = (P("ctx", "tp"), P("ctx", "tp", None))
    body = functools.partial(on_device, mesh.shape["ctx"], mesh.shape["tp"])
    return jax.shard_map(body, mesh=mesh, in_specs=in_specs, out_specs=out_specs, check_vma=False)
```

```python
import functools

import jax
import jax.numpy as jnp
from jax import lax
from jax.experimental import pallas as pl
from jax.experimental.pallas import tpu as pltpu
from jax.sharding import PartitionSpec as P

STATE = 16
DT_RANK = 512
MESH = pl.DeviceIdType.MESH
BF16 = jnp.bfloat16
F32 = jnp.float32


def dot(a, b):
    return jnp.dot(a, b, preferred_element_type=F32)


def dot_t(a, b):
    return lax.dot_general(a, b, (((1,), (1,)), ((), ())), preferred_element_type=F32)


def silu(v):
    return v * jax.nn.sigmoid(v)


def plane_sides(n_tp):
    chips = n_tp // 2
    side = 1
    while side * side < chips:
        side *= 2
    return chips // side, side


def kernel(
    n_ctx, n_tp, tokens_hbm, iw_hbm, gw_hbm, cw_hbm, cb_hbm, pw_hbm, sw_hbm, sb_hbm, dr_hbm, sg_hbm, ow_hbm, cs_hbm,
    mixed, boundary,
    x_buf, iw, gw, ow, pw, sw, cw, cb, sb, sg, dr, cs, acc, gate, pad, tail_in,
    p_send, p_recv, p_more, p_res, step_ref, drive_ref, conv_ref, h_buf, b_chunk, c_chunk, state_out, state_in, q_buf, y_buf,
    part, sib_part, mine, s1_send, s1_a, s1_b, s2_send, s2_a, s2_b,
    load_sem, ctx_sem, own_send, own_recv, sib_send, sib_recv, tail_sem, red_sem, more_sem, res_sem, state_send, state_recv,
    rs_sib_send, rs_sib_recv, s1_send_sem, s1_a_sem, s1_b_sem, s2_send_sem, s2_a_sem, s2_b_sem,
):
    ny, nx = plane_sides(n_tp)
    chips = ny * nx
    rows, width = tokens_hbm.shape
    half = rows // 2
    s, me = lax.axis_index("ctx"), lax.axis_index("tp")
    core, chip = lax.rem(me, 2), me // 2
    cx, cy = lax.rem(chip, nx), chip // nx

    def chip_at(dx, dy):
        return lax.rem(cy + dy + ny, ny) * nx + lax.rem(cx + dx + nx, nx)

    def tp_at(dx, dy, other=False):
        return chip_at(dx, dy) * 2 + ((1 - core) if other else core)

    def remote(src, dst, send, recv, to, ctx=None):
        return pltpu.make_async_remote_copy(
            src_ref=src, dst_ref=dst, send_sem=send, recv_sem=recv,
            device_id=(s if ctx is None else ctx, to), device_id_type=MESH,
        )

    def await_recv(ref, sem):
        remote(ref, ref, sem, sem, me).wait_recv()

    def await_send(ref, sem):
        remote(ref, ref, sem, sem, me).wait_send()

    loads = []
    for k, (src, dst) in enumerate(
        [(tokens_hbm, x_buf.at[me]), (iw_hbm, iw), (gw_hbm, gw), (pw_hbm, pw), (sw_hbm, sw), (cw_hbm, cw), (cb_hbm, cb),
         (sb_hbm, sb), (sg_hbm, sg), (dr_hbm, dr), (cs_hbm, cs), (ow_hbm, ow)]
    ):
        loads.append(pltpu.make_async_copy(src, dst, load_sem.at[k]))
        loads[-1].start()

    barrier = pltpu.get_barrier_semaphore()
    greeted = [(d, 0) for d in range(1, nx)] + [(0, d) for d in range(1, ny)]
    for a, b in greeted:
        pl.semaphore_signal(barrier, inc=1, device_id=(s, tp_at(a, b)), device_id_type=MESH)
    pl.semaphore_signal(barrier, inc=1, device_id=(s, tp_at(0, 0, True)), device_id_type=MESH)
    beside = sorted({1, n_ctx - 1}) if n_ctx > 1 else []

    def signal_ctx(sem, by):
        pl.semaphore_signal(sem, inc=1, device_id=(lax.rem(s + by, n_ctx), me), device_id_type=MESH)

    for by in beside:
        signal_ctx(barrier, by)
    loads[0].wait()
    pl.semaphore_wait(barrier, len(greeted) + 1 + len(beside))
    rounds = []
    reach = 1
    while 2 * reach < n_ctx:
        rounds.append(reach)
        reach *= 2

    def greet_round(i):
        if i > 0 and i <= len(rounds):
            pl.semaphore_wait(ctx_sem.at[i - 1], 2)
        if i < len(rounds):
            for by in (rounds[i], n_ctx - rounds[i]):
                signal_ctx(ctx_sem.at[i], by)

    greet_round(0)

    top, bottom = pl.ds(0, half), pl.ds(half, half)
    far_first_x = sorted(range(1, nx), key=lambda d: -min(d, nx - d))
    far_first_y = sorted(range(1, ny), key=lambda d: -min(d, ny - d))
    near_x, near_y = far_first_x[::-1], far_first_y[::-1]

    def send_piece(piece, h, dx, dy, rx, ry):
        view = x_buf.at[piece, bottom if h else top]
        remote(view, view, own_send, own_recv.at[rx * ny + ry, h], tp_at(dx, dy)).start()

    def await_piece(rx, ry, h):
        view = x_buf.at[tp_at(-rx, -ry), bottom if h else top]
        await_recv(view, own_recv.at[rx * ny + ry, h])

    def to_sibling(rx, ry):
        view = x_buf.at[tp_at(-rx, -ry)]
        remote(view, view, sib_send, sib_recv.at[rx * ny + ry], tp_at(0, 0, True)).start()

    def from_sibling(rx, ry):
        await_recv(x_buf.at[tp_at(-rx, -ry, True)], sib_recv.at[rx * ny + ry])

    for k in range(max(nx, ny) - 1):
        if k < nx - 1:
            send_piece(me, 0, far_first_x[k], 0, far_first_x[k], 0)
        if k < ny - 1:
            send_piece(me, 1, 0, far_first_y[k], 0, far_first_y[k])
    to_sibling(0, 0)
    for k in range(max(nx, ny) - 1):
        if k < ny - 1:
            send_piece(me, 0, 0, far_first_y[k], 0, far_first_y[k])
        if k < nx - 1:
            send_piece(me, 1, far_first_x[k], 0, far_first_x[k], 0)

    def times(piece, weight):
        first = pl.multiple_of(piece * width, width)
        return dot(x_buf[piece], weight[pl.ds(first, width), :])

    def add_inner(pieces, fresh=False):
        total = sum(times(p, iw) for p in pieces)
        acc[...] = total if fresh else acc[...] + total

    for k in range(max(nx, ny) - 1):
        if k < nx - 1:
            d = near_x[k]
            await_piece(d, 0, 0)
            for e in far_first_y:
                send_piece(tp_at(-d, 0), 0, 0, e, d, e)
        if k < ny - 1:
            d = near_y[k]
            await_piece(0, d, 1)
            for e in far_first_x:
                send_piece(tp_at(0, -d), 1, e, 0, e, d)
    greet_round(1)
    for load in loads[1:]:
        load.wait()
    decay, carried = dr[...], cs[...]
    from_sibling(0, 0)
    add_inner([tp_at(0, 0), tp_at(0, 0, True)], fresh=True)

    waiting = []
    for k in range(max(nx, ny) - 1):
        group = []
        if k < nx - 1:
            group.append((near_x[k], 0))
        if k < ny - 1:
            group.append((0, near_y[k]))
        for rx, ry in group:
            await_piece(rx, ry, 1 if ry == 0 else 0)
            to_sibling(rx, ry)
        for rx, ry in waiting:
            from_sibling(rx, ry)
        add_inner([tp_at(-a, -b) for a, b in group] + [tp_at(-a, -b, True) for a, b in waiting])
        waiting = group
    rest = sorted(
        [(a, b) for a in range(1, nx) for b in range(1, ny)],
        key=lambda r: max(near_x.index(r[0]), near_y.index(r[1])) * 10 + near_x.index(r[0]) + near_y.index(r[1]),
    )
    for k in range(0, len(rest), 3):
        group = rest[k : k + 3]
        for rx, ry in group:
            await_piece(rx, ry, 0)
            await_piece(rx, ry, 1)
            to_sibling(rx, ry)
        for rx, ry in waiting:
            from_sibling(rx, ry)
        add_inner([tp_at(-a, -b) for a, b in group] + [tp_at(-a, -b, True) for a, b in waiting])
        waiting = group
    for rx, ry in waiting:
        from_sibling(rx, ry)
    add_inner([tp_at(-a, -b, True) for a, b in waiting])

    for i in range(2, len(rounds) + 1):
        greet_round(i)

    pad[8:, :] = acc[...].astype(BF16).astype(F32)
    tail = pad.at[pl.ds(rows, 8)]
    first_shard = s == 0

    @pl.when(s < n_ctx - 1)
    def _():
        remote(tail, tail_in, tail_sem.at[0], tail_sem.at[1], me, ctx=lax.rem(s + 1, n_ctx)).start()

    gate[...] = sum(times(p, gw) for p in range(n_tp)).astype(BF16).astype(F32)

    @pl.when(first_shard)
    def _():
        tail_in[...] = jnp.zeros_like(tail_in)

    @pl.when(s > 0)
    def _():
        await_recv(tail_in, tail_sem.at[1])

    pad[0:8, :] = tail_in[...]
    taps = cw.shape[0]
    summed = cb[...] + cw[0:1, :] * pad[9 - taps : 9 - taps + rows, :]
    for k in range(1, taps):
        summed = summed + cw[k : k + 1, :] * pad[9 - taps + k : 9 - taps + k + rows, :]
    conv_low = silu(summed).astype(BF16)
    conv_ref[...] = conv_low.astype(F32)

    each = p_send.shape[1]
    proj = dot_t(conv_low, pw[:DT_RANK, :]).astype(BF16)
    across = DT_RANK // 128
    for block in range(n_tp * each):
        r, c = block // across, block % across
        p_send[block // each, block % each] = proj[r * 16 : r * 16 + 16, c * 128 : c * 128 + 128]
    bc = dot_t(pw[DT_RANK:, :], conv_low).astype(BF16)
    p_more[0, me] = bc[:STATE]
    p_more[1, me] = bc[STATE:]
    owners = (0, n_tp // 2)
    others = [(a, b, o) for a in range(nx) for b in range(ny) for o in (False, True) if a or b or o]
    others.sort(key=lambda r: -(min(r[0], nx - r[0]) + min(r[1], ny - r[1])))
    for a, b, other in others:
        to = tp_at(a, b, other)
        remote(p_send.at[to], p_recv.at[me], red_sem.at[0], red_sem.at[1], to).start()
    for which, owner in enumerate(owners):
        mine_too = p_more.at[which, me]

        @pl.when(me != owner)
        def _():
            remote(mine_too, mine_too, more_sem.at[which, 0], more_sem.at[which, 1], owner).start()

    p_recv[me] = p_send[me]
    await_recv(p_recv.at[pl.ds(0, n_tp - 1)], red_sem.at[1])
    total = p_recv[0].astype(F32)
    for i in range(1, n_tp):
        total = total + p_recv[i].astype(F32)
    p_res[pl.ds(me * each, each)] = total.astype(BF16)
    result = p_res.at[pl.ds(me * each, each)]
    for a, b, other in others:
        remote(result, result, res_sem.at[0], res_sem.at[1], tp_at(a, b, other)).start()
    blocks = n_tp * each
    for which, owner in enumerate(owners):
        place = p_res.at[pl.ds(blocks + which, 1)]

        @pl.when(me == owner)
        def _():
            await_recv(p_more.at[which, pl.ds(0, n_tp - 1)], more_sem.at[which, 1])
            total = p_more[which, 0].astype(F32)
            for i in range(1, n_tp):
                total = total + p_more[which, i].astype(F32)
            p_res[blocks + which] = total.astype(BF16)
            for i in range(1, n_tp):
                remote(place, place, more_sem.at[which, 2], more_sem.at[which, 3], lax.rem(me + i, n_tp)).start()

    await_recv(p_res.at[pl.ds(0, (n_tp - 1) * each)], res_sem.at[1])
    low = jnp.concatenate(
        [jnp.concatenate([p_res[r * across + c] for c in range(across)], axis=1) for r in range(rows // 16)], axis=0
    )
    step = jax.nn.softplus(dot(low, sw[...]) + sb[...])
    step_ref[...] = step
    drive_ref[...] = step * conv_ref[...]
    later = lax.broadcasted_iota(jnp.int32, (rows, rows), 0)
    earlier = lax.broadcasted_iota(jnp.int32, (rows, rows), 1)
    below = (earlier <= later).astype(F32)
    so_far = jnp.dot(below, step, preferred_element_type=F32, precision=lax.Precision.HIGHEST)

    for which, owner in enumerate(owners):

        @pl.when(me != owner)
        def _():
            await_recv(p_res.at[pl.ds(blocks + which, 1)], more_sem.at[which, 3])

    b_t, c_t = p_res[blocks].astype(F32), p_res[blocks + 1].astype(F32)
    run = 16
    for k in range(rows // run):
        turn = (rows - k * run) % rows
        b_chunk[k] = pltpu.roll(b_t, turn, 1) if turn else b_t
        c_chunk[k] = pltpu.roll(c_t, turn, 1) if turn else c_t

    def scan_chunk(k, h):
        first = pl.multiple_of(k * run, run)
        steps, drives, bs = step_ref[pl.ds(first, run), :], drive_ref[pl.ds(first, run), :], b_chunk[k]
        for i in range(run):
            h = jnp.exp(-steps[i : i + 1, :] * decay) * h + drives[i : i + 1, :] * bs[:, i : i + 1]
            h_buf[first + i] = h
        return h

    end = lax.fori_loop(0, rows // run, scan_chunk, jnp.zeros((STATE, width), F32))

    state_out[0:STATE, :] = end
    state_out[STATE:, :] = jnp.broadcast_to(so_far[rows - 1 :, :], (8, width))
    for d in range(1, n_ctx):

        @pl.when(s + d < n_ctx)
        def _():
            remote(
                state_out, state_in.at[n_ctx - 1 - d], state_send.at[d], state_recv.at[d], me, ctx=lax.rem(s + d, n_ctx)
            ).start()

    def read_chunk(k, carry):
        first = pl.multiple_of(k * run, run)
        c_now = c_chunk[k]
        lines = []
        for i in range(run):
            lines.append(jnp.sum(h_buf[first + i] * c_now[:, i : i + 1], axis=0, keepdims=True))
        y_buf[pl.ds(first, run), :] = jnp.concatenate(lines, axis=0)
        return carry

    lax.fori_loop(0, rows // run, read_chunk, 0)
    c_rows = jnp.transpose(c_t)
    for n in range(STATE):
        q_buf[n] = c_rows[:, n : n + 1] * jnp.exp(-so_far * decay[n : n + 1, :])
    y_buf[...] = y_buf[...] + sg[...] * conv_ref[...]
    gate[...] = silu(gate[...])

    for d in range(1, n_ctx):

        @pl.when(s >= d)
        def _():
            await_recv(state_in.at[n_ctx - 1 - d], state_recv.at[d])

    def enter(i, e):
        got = state_in[i]
        return jnp.exp(-decay * got[STATE : STATE + 1, :]) * e + got[:STATE, :]

    entering = lax.fori_loop(n_ctx - 1 - s, n_ctx - 1, enter, carried)
    boundary[...] = jnp.exp(-decay * state_out[STATE : STATE + 1, :]) * entering + end

    readout = y_buf[...]
    for n in range(STATE):
        readout = readout + q_buf[n] * entering[n : n + 1, :]
    gated = (readout * gate[...]).astype(BF16)

    def out_piece(piece):
        first = pl.multiple_of(piece * width, width)
        return dot(gated, ow[:, pl.ds(first, width)])

    def combine(ex, ey):
        r = ex * ny + ey
        await_recv(sib_part.at[r], rs_sib_recv.at[r])
        total = mine[r] + sib_part[r].astype(F32)
        mine[r] = total
        s1_send[r] = total.astype(BF16)
        if ey:
            remote(s1_send.at[r, top], s1_a.at[ey, ex], s1_send_sem, s1_a_sem.at[ey, ex], tp_at(0, ey)).start()
        if ex:
            remote(s1_send.at[r, bottom], s1_b.at[ex, ey], s1_send_sem, s1_b_sem.at[ex, ey], tp_at(ex, 0)).start()

    order = [(a, b) for a in far_first_x for b in far_first_y]
    order += [(0, b) for b in far_first_y] + [(a, 0) for a in far_first_x] + [(0, 0)]
    lag = 2
    for k, (ex, ey) in enumerate(order):
        r = ex * ny + ey
        part[r] = out_piece(tp_at(ex, ey, True)).astype(BF16)
        remote(part.at[r], sib_part.at[r], rs_sib_send, rs_sib_recv.at[r], tp_at(0, 0, True)).start()
        mine[r] = out_piece(tp_at(ex, ey))
        if k >= lag:
            combine(*order[k - lag])
    for k in range(max(0, len(order) - lag), len(order)):
        combine(*order[k])

    def second_a(ex):
        total = mine[ex * ny, top, :]
        for e in range(1, ny):
            await_recv(s1_a.at[e, ex], s1_a_sem.at[e, ex])
            total = total + s1_a[e, ex].astype(F32)
        return total

    def second_b(ey):
        total = mine[ey, bottom, :]
        for e in range(1, nx):
            await_recv(s1_b.at[e, ey], s1_b_sem.at[e, ey])
            total = total + s1_b[e, ey].astype(F32)
        return total

    for k in range(max(nx, ny) - 1):
        if k < nx - 1:
            d = far_first_x[k]
            s2_send[0, d] = second_a(d).astype(BF16)
            remote(s2_send.at[0, d], s2_a.at[d], s2_send_sem.at[0, d], s2_a_sem.at[d], tp_at(d, 0)).start()
        if k < ny - 1:
            d = far_first_y[k]
            s2_send[1, d] = second_b(d).astype(BF16)
            remote(s2_send.at[1, d], s2_b.at[d], s2_send_sem.at[1, d], s2_b_sem.at[d], tp_at(0, d)).start()
    upper, lower = second_a(0), second_b(0)
    for d in near_x:
        await_recv(s2_a.at[d], s2_a_sem.at[d])
        upper = upper + s2_a[d].astype(F32)
    mixed[0:half, :] = upper.astype(BF16)
    for d in near_y:
        await_recv(s2_b.at[d], s2_b_sem.at[d])
        lower = lower + s2_b[d].astype(F32)
    mixed[half:, :] = lower.astype(BF16)

    await_send(x_buf.at[pl.ds(0, chips - 1)], own_send)
    await_send(x_buf.at[pl.ds(0, chips)], sib_send)

    @pl.when(s < n_ctx - 1)
    def _():
        await_send(tail, tail_sem.at[0])

    await_send(p_recv.at[pl.ds(0, n_tp - 1)], red_sem.at[0])
    await_send(p_res.at[pl.ds(0, (n_tp - 1) * each)], res_sem.at[0])
    for which, owner in enumerate(owners):

        @pl.when(me != owner)
        def _():
            await_send(p_more.at[which, 0], more_sem.at[which, 0])

        @pl.when(me == owner)
        def _():
            await_send(p_more.at[which, pl.ds(0, n_tp - 1)], more_sem.at[which, 2])

    for d in range(1, n_ctx):

        @pl.when(s + d < n_ctx)
        def _():
            await_send(state_out, state_send.at[d])

    await_send(sib_part, rs_sib_send)
    for a in range(nx):
        for b in range(ny):
            if b:
                await_send(s1_send.at[0, top], s1_send_sem)
            if a:
                await_send(s1_send.at[0, top], s1_send_sem)
    for d in range(1, nx):
        await_send(s2_send.at[0, d], s2_send_sem.at[0, d])
    for d in range(1, ny):
        await_send(s2_send.at[1, d], s2_send_sem.at[1, d])


def hand_on(a_in, b_in, a_out, b_out):
    a_out[...] = a_in[...]
    b_out[...] = b_in[...]


def on_device(
    n_ctx, n_tp, tokens, inner_weight, gate_weight, conv_weight, conv_bias, proj_weight, step_weight, step_bias, decay_rate,
    skip_gain, out_weight, carried_state,
):
    rows, width = tokens.shape
    depth = inner_weight.shape[0]
    ny, nx = plane_sides(n_tp)
    chips = ny * nx
    half = rows // 2
    each = (rows // 16) * (DT_RANK // 128) // n_tp
    vmem, dma = pltpu.VMEM, pltpu.SemaphoreType.DMA
    args = (
        tokens, inner_weight, gate_weight, conv_weight, conv_bias[None, :], jnp.transpose(proj_weight), step_weight,
        step_bias[None, :], jnp.transpose(decay_rate), skip_gain[None, :], out_weight, jnp.transpose(carried_state),
    )
    held = (inner_weight, gate_weight, out_weight, args[5], step_weight, conv_weight)
    mixed, boundary = pl.pallas_call(
        functools.partial(kernel, n_ctx, n_tp),
        out_shape=(
            jax.ShapeDtypeStruct((rows, width), BF16),
            jax.ShapeDtypeStruct((STATE, width), F32),
        ),
        in_specs=[pl.BlockSpec(memory_space=pl.ANY)] * len(args),
        out_specs=[pl.BlockSpec(memory_space=pltpu.VMEM)] * 2,
        scratch_shapes=[
            vmem((n_tp, rows, width), BF16),
            *[vmem(a.shape, a.dtype) for a in held],
            *[vmem((1, width), F32)] * 3,
            *[vmem((STATE, width), F32)] * 2,
            *[vmem((rows, width), F32)] * 2,
            vmem((rows + 8, width), F32),
            vmem((8, width), F32),
            vmem((n_tp, each, 16, 128), BF16),
            vmem((n_tp, each, 16, 128), BF16),
            vmem((2, n_tp, STATE, 128), BF16),
            vmem((n_tp * each + 2, 16, 128), BF16),
            *[vmem((rows, width), F32)] * 3,
            vmem((rows, STATE, width), F32),
            *[vmem((rows // 16, STATE, rows), F32)] * 2,
            vmem((STATE + 8, width), F32),
            vmem((n_ctx, STATE + 8, width), F32),
            vmem((STATE, rows, width), F32),
            vmem((rows, width), F32),
            *[vmem((chips, rows, width), BF16)] * 2,
            vmem((chips, rows, width), F32),
            vmem((chips, rows, width), BF16),
            vmem((ny, nx, half, width), BF16),
            vmem((nx, ny, half, width), BF16),
            vmem((2, max(nx, ny), half, width), BF16),
            vmem((nx, half, width), BF16),
            vmem((ny, half, width), BF16),
            dma((len(args),)),
            pltpu.SemaphoreType.REGULAR((4,)),
            dma,
            dma((chips, 2)),
            dma,
            dma((chips,)),
            dma((2,)),
            dma((2,)),
            dma((2, 4)),
            dma((2,)),
            dma((n_ctx,)),
            dma((n_ctx,)),
            dma,
            dma((chips,)),
            dma,
            dma((ny, nx)),
            dma((nx, ny)),
            dma((2, max(nx, ny))),
            dma((nx,)),
            dma((ny,)),
        ],
        compiler_params=pltpu.CompilerParams(collective_id=0, has_side_effects=True, vmem_limit_bytes=56 << 20),
        cost_estimate=pl.CostEstimate(
            flops=2 * rows * width * (3 * depth + 544 + 512), bytes_accessed=3 * depth * width * 2, transcendentals=0
        ),
        name="layer",
    )(*args)
    mixed, boundary = pl.pallas_call(
        hand_on,
        out_shape=(
            jax.ShapeDtypeStruct((rows, width), BF16),
            jax.ShapeDtypeStruct((STATE, width), F32),
        ),
        in_specs=[pl.BlockSpec(memory_space=pltpu.VMEM)] * 2,
        out_specs=[pl.BlockSpec(memory_space=pltpu.VMEM)] * 2,
        cost_estimate=pl.CostEstimate(flops=0, bytes_accessed=4 * rows * width, transcendentals=0),
        name="results",
    )(mixed, boundary)
    return mixed, jnp.transpose(boundary)[None]


def solution(mesh):
    in_specs = (
        P("ctx", "tp"), P(None, "tp"), P(None, "tp"), P(None, "tp"), P("tp"), P("tp", None), P(None, "tp"), P("tp"),
        P("tp", None), P("tp"), P("tp", None), P("tp", None),
    )
    out_specs = (P("ctx", "tp"), P("ctx", "tp", None))
    body = functools.partial(on_device, mesh.shape["ctx"], mesh.shape["tp"])
    return jax.shard_map(body, mesh=mesh, in_specs=in_specs, out_specs=out_specs, check_vma=False)
```

```python
import functools

import jax
import jax.numpy as jnp
from jax import lax
from jax.experimental import pallas as pl
from jax.experimental.pallas import tpu as pltpu
from jax.sharding import PartitionSpec as P

STATE = 16
DT_RANK = 512
MESH = pl.DeviceIdType.MESH
BF16 = jnp.bfloat16
F32 = jnp.float32


def dot(a, b):
    return jnp.dot(a, b, preferred_element_type=F32)


def dot_t(a, b):
    return lax.dot_general(a, b, (((1,), (1,)), ((), ())), preferred_element_type=F32)


def silu(v):
    return v * jax.nn.sigmoid(v)


def plane_sides(n_tp):
    chips = n_tp // 2
    side = 1
    while side * side < chips:
        side *= 2
    return chips // side, side


def kernel(
    n_ctx, n_tp, tokens_hbm, iw_hbm, gw_hbm, cw_hbm, cb_hbm, pw_hbm, sw_hbm, sb_hbm, dr_hbm, sg_hbm, ow_hbm, cs_hbm,
    mixed, boundary,
    x_buf, iw, gw, ow, pw, sw, cw, cb, sb, sg, dr, cs, acc, gate, pad, tail_in,
    p_send, p_recv, p_more, p_res, step_ref, drive_ref, conv_ref, h_buf, b_chunk, c_chunk, state_out, state_in, sums_out, sums_in, q_buf, y_buf,
    part, sib_part, mine, s1_send, s1_a, s1_b, s2_send, s2_a, s2_b,
    load_sem, ctx_sem, own_send, own_recv, sib_send, sib_recv, tail_sem, red_sem, more_sem, res_sem, state_send, state_recv,
    rs_sib_send, rs_sib_recv, s1_send_sem, s1_a_sem, s1_b_sem, s2_send_sem, s2_a_sem, s2_b_sem,
):
    ny, nx = plane_sides(n_tp)
    chips = ny * nx
    rows, width = tokens_hbm.shape
    half = rows // 2
    s, me = lax.axis_index("ctx"), lax.axis_index("tp")
    core, chip = lax.rem(me, 2), me // 2
    cx, cy = lax.rem(chip, nx), chip // nx

    def chip_at(dx, dy):
        return lax.rem(cy + dy + ny, ny) * nx + lax.rem(cx + dx + nx, nx)

    def tp_at(dx, dy, other=False):
        return chip_at(dx, dy) * 2 + ((1 - core) if other else core)

    def remote(src, dst, send, recv, to, ctx=None):
        return pltpu.make_async_remote_copy(
            src_ref=src, dst_ref=dst, send_sem=send, recv_sem=recv,
            device_id=(s if ctx is None else ctx, to), device_id_type=MESH,
        )

    def await_recv(ref, sem):
        remote(ref, ref, sem, sem, me).wait_recv()

    def await_send(ref, sem):
        remote(ref, ref, sem, sem, me).wait_send()

    barrier = pltpu.get_barrier_semaphore()
    greeted = [(d, 0) for d in range(1, nx)] + [(0, d) for d in range(1, ny)]
    for a, b in greeted:
        pl.semaphore_signal(barrier, inc=1, device_id=(s, tp_at(a, b)), device_id_type=MESH)
    pl.semaphore_signal(barrier, inc=1, device_id=(s, tp_at(0, 0, True)), device_id_type=MESH)
    beside = sorted({1, n_ctx - 1}) if n_ctx > 1 else []

    def signal_ctx(sem, by):
        pl.semaphore_signal(sem, inc=1, device_id=(lax.rem(s + by, n_ctx), me), device_id_type=MESH)

    for by in beside:
        signal_ctx(barrier, by)

    loads = []
    for k, (src, dst) in enumerate(
        [(tokens_hbm, x_buf.at[me]), (iw_hbm, iw), (gw_hbm, gw), (pw_hbm, pw), (sw_hbm, sw), (cw_hbm, cw), (cb_hbm, cb),
         (sb_hbm, sb), (sg_hbm, sg), (dr_hbm, dr), (cs_hbm, cs), (ow_hbm, ow)]
    ):
        loads.append(pltpu.make_async_copy(src, dst, load_sem.at[k]))
        loads[-1].start()

    loads[0].wait()
    pl.semaphore_wait(barrier, len(greeted) + 1 + len(beside))
    rounds = []
    reach = 1
    while 2 * reach < n_ctx:
        rounds.append(reach)
        reach *= 2

    def greet_round(i):
        if i > 0 and i <= len(rounds):
            pl.semaphore_wait(ctx_sem.at[i - 1], 2)
        if i < len(rounds):
            for by in (rounds[i], n_ctx - rounds[i]):
                signal_ctx(ctx_sem.at[i], by)

    greet_round(0)

    top, bottom = pl.ds(0, half), pl.ds(half, half)
    far_first_x = sorted(range(1, nx), key=lambda d: -min(d, nx - d))
    far_first_y = sorted(range(1, ny), key=lambda d: -min(d, ny - d))
    near_x, near_y = far_first_x[::-1], far_first_y[::-1]

    def send_piece(piece, h, dx, dy, rx, ry):
        view = x_buf.at[piece, bottom if h else top]
        remote(view, view, own_send, own_recv.at[rx * ny + ry, h], tp_at(dx, dy)).start()

    def await_piece(rx, ry, h):
        view = x_buf.at[tp_at(-rx, -ry), bottom if h else top]
        await_recv(view, own_recv.at[rx * ny + ry, h])

    def to_sibling(rx, ry):
        view = x_buf.at[tp_at(-rx, -ry)]
        remote(view, view, sib_send, sib_recv.at[rx * ny + ry], tp_at(0, 0, True)).start()

    def from_sibling(rx, ry):
        await_recv(x_buf.at[tp_at(-rx, -ry, True)], sib_recv.at[rx * ny + ry])

    for k in range(max(nx, ny) - 1):
        if k < nx - 1:
            send_piece(me, 0, far_first_x[k], 0, far_first_x[k], 0)
        if k < ny - 1:
            send_piece(me, 1, 0, far_first_y[k], 0, far_first_y[k])
    to_sibling(0, 0)
    for k in range(max(nx, ny) - 1):
        if k < ny - 1:
            send_piece(me, 0, 0, far_first_y[k], 0, far_first_y[k])
        if k < nx - 1:
            send_piece(me, 1, far_first_x[k], 0, far_first_x[k], 0)

    def times(piece, weight):
        first = pl.multiple_of(piece * width, width)
        return dot(x_buf[piece], weight[pl.ds(first, width), :])

    def add_inner(pieces, fresh=False):
        total = sum(times(p, iw) for p in pieces)
        acc[...] = total if fresh else acc[...] + total

    for k in range(max(nx, ny) - 1):
        if k < nx - 1:
            d = near_x[k]
            await_piece(d, 0, 0)
            for e in far_first_y:
                send_piece(tp_at(-d, 0), 0, 0, e, d, e)
        if k < ny - 1:
            d = near_y[k]
            await_piece(0, d, 1)
            for e in far_first_x:
                send_piece(tp_at(0, -d), 1, e, 0, e, d)
    greet_round(1)
    for load in loads[1:]:
        load.wait()
    decay, carried = dr[...], cs[...]
    from_sibling(0, 0)
    add_inner([tp_at(0, 0), tp_at(0, 0, True)], fresh=True)

    waiting = []
    for k in range(max(nx, ny) - 1):
        group = []
        if k < nx - 1:
            group.append((near_x[k], 0))
        if k < ny - 1:
            group.append((0, near_y[k]))
        for rx, ry in group:
            await_piece(rx, ry, 1 if ry == 0 else 0)
            to_sibling(rx, ry)
        for rx, ry in waiting:
            from_sibling(rx, ry)
        add_inner([tp_at(-a, -b) for a, b in group] + [tp_at(-a, -b, True) for a, b in waiting])
        waiting = group
    rest = sorted(
        [(a, b) for a in range(1, nx) for b in range(1, ny)],
        key=lambda r: max(near_x.index(r[0]), near_y.index(r[1])) * 10 + near_x.index(r[0]) + near_y.index(r[1]),
    )
    for k in range(0, len(rest), 3):
        group = rest[k : k + 3]
        for rx, ry in group:
            await_piece(rx, ry, 0)
            await_piece(rx, ry, 1)
            to_sibling(rx, ry)
        for rx, ry in waiting:
            from_sibling(rx, ry)
        add_inner([tp_at(-a, -b) for a, b in group] + [tp_at(-a, -b, True) for a, b in waiting])
        waiting = group
    for rx, ry in waiting:
        from_sibling(rx, ry)
    add_inner([tp_at(-a, -b, True) for a, b in waiting])

    for i in range(2, len(rounds) + 1):
        greet_round(i)

    pad[8:, :] = acc[...].astype(BF16).astype(F32)
    tail = pad.at[pl.ds(rows, 8)]
    first_shard = s == 0

    @pl.when(s < n_ctx - 1)
    def _():
        remote(tail, tail_in, tail_sem.at[0], tail_sem.at[1], me, ctx=lax.rem(s + 1, n_ctx)).start()

    taps = cw.shape[0]
    each = p_send.shape[1]
    across = DT_RANK // 128
    early = across // each
    others = [(a, b, o) for a in range(nx) for b in range(ny) for o in (False, True) if a or b or o]
    others.sort(key=lambda r: -(min(r[0], nx - r[0]) + min(r[1], ny - r[1])))

    def convolve(first, count):
        summed = cb[...] + cw[0:1, :] * pad[9 - taps + first : 9 - taps + first + count, :]
        for k in range(1, taps):
            summed = summed + cw[k : k + 1, :] * pad[9 - taps + first + k : 9 - taps + first + k + count, :]
        low_bits = silu(summed).astype(BF16)
        conv_ref[first : first + count, :] = low_bits.astype(F32)
        return low_bits

    def project(first, conv_low):
        proj = dot_t(conv_low, pw[:DT_RANK, :]).astype(BF16)
        for r in range(first // 16, (first + conv_low.shape[0]) // 16):
            for c in range(across):
                block, at = r * across + c, r * 16 - first
                p_send[block // each, block % each] = proj[at : at + 16, c * 128 : c * 128 + 128]

    def send_block(to):
        remote(p_send.at[to], p_recv.at[me], red_sem.at[0], red_sem.at[1], to).start()

    conv_rest = convolve(16, rows - 16)
    project(16, conv_rest)
    for a, b, other in others:
        to = tp_at(a, b, other)
        pl.when(to >= early)(functools.partial(send_block, to))

    gate[...] = sum(times(p, gw) for p in range(n_tp)).astype(BF16).astype(F32)

    @pl.when(first_shard)
    def _():
        tail_in[...] = jnp.zeros_like(tail_in)

    @pl.when(s > 0)
    def _():
        await_recv(tail_in, tail_sem.at[1])

    pad[0:8, :] = tail_in[...]
    conv_first = convolve(0, 16)
    project(0, conv_first)
    for to in range(early):
        pl.when(me != to)(functools.partial(send_block, to))

    bc = dot_t(pw[DT_RANK:, :], jnp.concatenate([conv_first, conv_rest], axis=0)).astype(BF16)
    p_more[0, me] = bc[:STATE]
    p_more[1, me] = bc[STATE:]
    owners = (0, n_tp // 2)
    for which, owner in enumerate(owners):
        mine_too = p_more.at[which, me]

        @pl.when(me != owner)
        def _():
            remote(mine_too, mine_too, more_sem.at[which, 0], more_sem.at[which, 1], owner).start()

    p_recv[me] = p_send[me]
    await_recv(p_recv.at[pl.ds(0, n_tp - 1)], red_sem.at[1])
    total = p_recv[0].astype(F32)
    for i in range(1, n_tp):
        total = total + p_recv[i].astype(F32)
    p_res[pl.ds(me * each, each)] = total.astype(BF16)
    result = p_res.at[pl.ds(me * each, each)]
    for a, b, other in others:
        remote(result, result, res_sem.at[0], res_sem.at[1], tp_at(a, b, other)).start()
    blocks = n_tp * each
    for which, owner in enumerate(owners):
        place = p_res.at[pl.ds(blocks + which, 1)]

        @pl.when(me == owner)
        def _():
            await_recv(p_more.at[which, pl.ds(0, n_tp - 1)], more_sem.at[which, 1])
            total = p_more[which, 0].astype(F32)
            for i in range(1, n_tp):
                total = total + p_more[which, i].astype(F32)
            p_res[blocks + which] = total.astype(BF16)
            for i in range(1, n_tp):
                remote(place, place, more_sem.at[which, 2], more_sem.at[which, 3], lax.rem(me + i, n_tp)).start()

    await_recv(p_res.at[pl.ds(0, (n_tp - 1) * each)], res_sem.at[1])
    low = jnp.concatenate(
        [jnp.concatenate([p_res[r * across + c] for c in range(across)], axis=1) for r in range(rows // 16)], axis=0
    )
    step = jax.nn.softplus(dot(low, sw[...]) + sb[...])
    step_ref[...] = step
    drive_ref[...] = step * conv_ref[...]
    later = lax.broadcasted_iota(jnp.int32, (rows, rows), 0)
    earlier = lax.broadcasted_iota(jnp.int32, (rows, rows), 1)
    below = (earlier <= later).astype(F32)
    so_far = jnp.dot(below, step, preferred_element_type=F32, precision=lax.Precision.HIGHEST)

    for which, owner in enumerate(owners):

        @pl.when(me != owner)
        def _():
            await_recv(p_res.at[pl.ds(blocks + which, 1)], more_sem.at[which, 3])

    b_t, c_t = p_res[blocks].astype(F32), p_res[blocks + 1].astype(F32)
    run = 16
    for k in range(rows // run):
        turn = (rows - k * run) % rows
        b_chunk[k] = pltpu.roll(b_t, turn, 1) if turn else b_t
        c_chunk[k] = pltpu.roll(c_t, turn, 1) if turn else c_t

    def scan_chunk(k, h):
        first = pl.multiple_of(k * run, run)
        steps, drives, bs = step_ref[pl.ds(first, run), :], drive_ref[pl.ds(first, run), :], b_chunk[k]
        for i in range(run):
            h = jnp.exp(-steps[i : i + 1, :] * decay) * h + drives[i : i + 1, :] * bs[:, i : i + 1]
            h_buf[first + i] = h
        return h

    end = lax.fori_loop(0, rows // run, scan_chunk, jnp.zeros((STATE, width), F32))

    state_out[...] = end.astype(BF16)
    sums_out[...] = so_far[rows - 1 :, :]
    for d in sorted(range(1, n_ctx), key=lambda d: -min(d, n_ctx - d)):

        @pl.when(s + d < n_ctx)
        def _():
            to, slot = lax.rem(s + d, n_ctx), n_ctx - 1 - d
            remote(state_out, state_in.at[slot], state_send.at[d, 0], state_recv.at[d, 0], me, ctx=to).start()
            remote(sums_out, sums_in.at[slot], state_send.at[d, 1], state_recv.at[d, 1], me, ctx=to).start()

    def read_chunk(k, carry):
        first = pl.multiple_of(k * run, run)
        c_now = c_chunk[k]
        lines = []
        for i in range(run):
            lines.append(jnp.sum(h_buf[first + i] * c_now[:, i : i + 1], axis=0, keepdims=True))
        y_buf[pl.ds(first, run), :] = jnp.concatenate(lines, axis=0)
        return carry

    lax.fori_loop(0, rows // run, read_chunk, 0)
    c_rows = jnp.transpose(c_t)
    for n in range(STATE):
        q_buf[n] = c_rows[:, n : n + 1] * jnp.exp(-so_far * decay[n : n + 1, :])
    y_buf[...] = y_buf[...] + sg[...] * conv_ref[...]
    gate[...] = silu(gate[...])

    for d in range(1, n_ctx):

        @pl.when(s >= d)
        def _():
            await_recv(state_in.at[n_ctx - 1 - d], state_recv.at[d, 0])
            await_recv(sums_in.at[n_ctx - 1 - d], state_recv.at[d, 1])

    def enter(i, e):
        return jnp.exp(-decay * sums_in[i]) * e + state_in[i].astype(F32)

    entering = lax.fori_loop(n_ctx - 1 - s, n_ctx - 1, enter, carried)
    boundary[...] = jnp.exp(-decay * sums_out[...]) * entering + end

    readout = y_buf[...]
    for n in range(STATE):
        readout = readout + q_buf[n] * entering[n : n + 1, :]
    gated = (readout * gate[...]).astype(BF16)

    def out_piece(piece):
        first = pl.multiple_of(piece * width, width)
        return dot(gated, ow[:, pl.ds(first, width)])

    def combine(ex, ey):
        r = ex * ny + ey
        await_recv(sib_part.at[r], rs_sib_recv.at[r])
        total = mine[r] + sib_part[r].astype(F32)
        mine[r] = total
        s1_send[r] = total.astype(BF16)
        if ey:
            remote(s1_send.at[r, top], s1_a.at[ey, ex], s1_send_sem, s1_a_sem.at[ey, ex], tp_at(0, ey)).start()
        if ex:
            remote(s1_send.at[r, bottom], s1_b.at[ex, ey], s1_send_sem, s1_b_sem.at[ex, ey], tp_at(ex, 0)).start()

    order = sorted(
        [(a, b) for a in far_first_x for b in far_first_y],
        key=lambda r: (min(far_first_x.index(r[0]), far_first_y.index(r[1])), far_first_x.index(r[0]) + far_first_y.index(r[1])),
    )
    order += [(0, b) for b in far_first_y] + [(a, 0) for a in far_first_x] + [(0, 0)]
    lag = 2
    for k, (ex, ey) in enumerate(order):
        r = ex * ny + ey
        part[r] = out_piece(tp_at(ex, ey, True)).astype(BF16)
        remote(part.at[r], sib_part.at[r], rs_sib_send, rs_sib_recv.at[r], tp_at(0, 0, True)).start()
        mine[r] = out_piece(tp_at(ex, ey))
        if k >= lag:
            combine(*order[k - lag])
    for k in range(max(0, len(order) - lag), len(order)):
        combine(*order[k])

    def second_a(ex):
        total = mine[ex * ny, top, :]
        for e in range(1, ny):
            await_recv(s1_a.at[e, ex], s1_a_sem.at[e, ex])
            total = total + s1_a[e, ex].astype(F32)
        return total

    def second_b(ey):
        total = mine[ey, bottom, :]
        for e in range(1, nx):
            await_recv(s1_b.at[e, ey], s1_b_sem.at[e, ey])
            total = total + s1_b[e, ey].astype(F32)
        return total

    for k in range(max(nx, ny) - 1):
        if k < nx - 1:
            d = far_first_x[k]
            s2_send[0, d] = second_a(d).astype(BF16)
            remote(s2_send.at[0, d], s2_a.at[d], s2_send_sem.at[0, d], s2_a_sem.at[d], tp_at(d, 0)).start()
        if k < ny - 1:
            d = far_first_y[k]
            s2_send[1, d] = second_b(d).astype(BF16)
            remote(s2_send.at[1, d], s2_b.at[d], s2_send_sem.at[1, d], s2_b_sem.at[d], tp_at(0, d)).start()
    upper, lower = second_a(0), second_b(0)
    for d in near_x:
        await_recv(s2_a.at[d], s2_a_sem.at[d])
        upper = upper + s2_a[d].astype(F32)
    mixed[0:half, :] = upper.astype(BF16)
    for d in near_y:
        await_recv(s2_b.at[d], s2_b_sem.at[d])
        lower = lower + s2_b[d].astype(F32)
    mixed[half:, :] = lower.astype(BF16)

    await_send(x_buf.at[pl.ds(0, chips - 1)], own_send)
    await_send(x_buf.at[pl.ds(0, chips)], sib_send)

    @pl.when(s < n_ctx - 1)
    def _():
        await_send(tail, tail_sem.at[0])

    await_send(p_recv.at[pl.ds(0, n_tp - 1)], red_sem.at[0])
    await_send(p_res.at[pl.ds(0, (n_tp - 1) * each)], res_sem.at[0])
    for which, owner in enumerate(owners):

        @pl.when(me != owner)
        def _():
            await_send(p_more.at[which, 0], more_sem.at[which, 0])

        @pl.when(me == owner)
        def _():
            await_send(p_more.at[which, pl.ds(0, n_tp - 1)], more_sem.at[which, 2])

    for d in range(1, n_ctx):

        @pl.when(s + d < n_ctx)
        def _():
            await_send(state_out, state_send.at[d, 0])
            await_send(sums_out, state_send.at[d, 1])

    await_send(sib_part, rs_sib_send)
    for a in range(nx):
        for b in range(ny):
            if b:
                await_send(s1_send.at[0, top], s1_send_sem)
            if a:
                await_send(s1_send.at[0, top], s1_send_sem)
    for d in range(1, nx):
        await_send(s2_send.at[0, d], s2_send_sem.at[0, d])
    for d in range(1, ny):
        await_send(s2_send.at[1, d], s2_send_sem.at[1, d])


def hand_on(a_in, b_in, a_out, b_out):
    a_out[...] = a_in[...]
    b_out[...] = b_in[...]


def on_device(
    n_ctx, n_tp, tokens, inner_weight, gate_weight, conv_weight, conv_bias, proj_weight, step_weight, step_bias, decay_rate,
    skip_gain, out_weight, carried_state,
):
    rows, width = tokens.shape
    depth = inner_weight.shape[0]
    ny, nx = plane_sides(n_tp)
    chips = ny * nx
    half = rows // 2
    each = (rows // 16) * (DT_RANK // 128) // n_tp
    vmem, dma = pltpu.VMEM, pltpu.SemaphoreType.DMA
    args = (
        tokens, inner_weight, gate_weight, conv_weight, conv_bias[None, :], jnp.transpose(proj_weight), step_weight,
        step_bias[None, :], jnp.transpose(decay_rate), skip_gain[None, :], out_weight, jnp.transpose(carried_state),
    )
    held = (inner_weight, gate_weight, out_weight, args[5], step_weight, conv_weight)
    mixed, boundary = pl.pallas_call(
        functools.partial(kernel, n_ctx, n_tp),
        out_shape=(
            jax.ShapeDtypeStruct((rows, width), BF16),
            jax.ShapeDtypeStruct((STATE, width), F32),
        ),
        in_specs=[pl.BlockSpec(memory_space=pl.ANY)] * len(args),
        out_specs=[pl.BlockSpec(memory_space=pltpu.VMEM)] * 2,
        scratch_shapes=[
            vmem((n_tp, rows, width), BF16),
            *[vmem(a.shape, a.dtype) for a in held],
            *[vmem((1, width), F32)] * 3,
            *[vmem((STATE, width), F32)] * 2,
            *[vmem((rows, width), F32)] * 2,
            vmem((rows + 8, width), F32),
            vmem((8, width), F32),
            vmem((n_tp, each, 16, 128), BF16),
            vmem((n_tp, each, 16, 128), BF16),
            vmem((2, n_tp, STATE, 128), BF16),
            vmem((n_tp * each + 2, 16, 128), BF16),
            *[vmem((rows, width), F32)] * 3,
            vmem((rows, STATE, width), F32),
            *[vmem((rows // 16, STATE, rows), F32)] * 2,
            vmem((STATE, width), BF16),
            vmem((n_ctx, STATE, width), BF16),
            vmem((1, width), F32),
            vmem((n_ctx, 1, width), F32),
            vmem((STATE, rows, width), F32),
            vmem((rows, width), F32),
            *[vmem((chips, rows, width), BF16)] * 2,
            vmem((chips, rows, width), F32),
            vmem((chips, rows, width), BF16),
            vmem((ny, nx, half, width), BF16),
            vmem((nx, ny, half, width), BF16),
            vmem((2, max(nx, ny), half, width), BF16),
            vmem((nx, half, width), BF16),
            vmem((ny, half, width), BF16),
            dma((len(args),)),
            pltpu.SemaphoreType.REGULAR((4,)),
            dma,
            dma((chips, 2)),
            dma,
            dma((chips,)),
            dma((2,)),
            dma((2,)),
            dma((2, 4)),
            dma((2,)),
            dma((n_ctx, 2)),
            dma((n_ctx, 2)),
            dma,
            dma((chips,)),
            dma,
            dma((ny, nx)),
            dma((nx, ny)),
            dma((2, max(nx, ny))),
            dma((nx,)),
            dma((ny,)),
        ],
        compiler_params=pltpu.CompilerParams(collective_id=0, has_side_effects=True, vmem_limit_bytes=56 << 20),
        cost_estimate=pl.CostEstimate(
            flops=2 * rows * width * (3 * depth + 544 + 512), bytes_accessed=3 * depth * width * 2, transcendentals=0
        ),
        name="layer",
    )(*args)
    mixed, boundary = pl.pallas_call(
        hand_on,
        out_shape=(
            jax.ShapeDtypeStruct((rows, width), BF16),
            jax.ShapeDtypeStruct((STATE, width), F32),
        ),
        in_specs=[pl.BlockSpec(memory_space=pltpu.VMEM)] * 2,
        out_specs=[pl.BlockSpec(memory_space=pltpu.VMEM)] * 2,
        cost_estimate=pl.CostEstimate(flops=0, bytes_accessed=4 * rows * width, transcendentals=0),
        name="results",
    )(mixed, boundary)
    return mixed, jnp.transpose(boundary)[None]


def solution(mesh):
    in_specs = (
        P("ctx", "tp"), P(None, "tp"), P(None, "tp"), P(None, "tp"), P("tp"), P("tp", None), P(None, "tp"), P("tp"),
        P("tp", None), P("tp"), P("tp", None), P("tp", None),
    )
    out_specs = (P("ctx", "tp"), P("ctx", "tp", None))
    body = functools.partial(on_device, mesh.shape["ctx"], mesh.shape["tp"])
    return jax.shard_map(body, mesh=mesh, in_specs=in_specs, out_specs=out_specs, check_vma=False)
```

```python
import functools

import jax
import jax.numpy as jnp
from jax import lax
from jax.experimental import pallas as pl
from jax.experimental.pallas import tpu as pltpu
from jax.sharding import PartitionSpec as P

STATE = 16
DT_RANK = 512
MESH = pl.DeviceIdType.MESH
BF16 = jnp.bfloat16
F32 = jnp.float32


def dot(a, b):
    return jnp.dot(a, b, preferred_element_type=F32)


def dot_t(a, b):
    return lax.dot_general(a, b, (((1,), (1,)), ((), ())), preferred_element_type=F32)


def silu(v):
    return v * jax.nn.sigmoid(v)


def plane_sides(n_tp):
    chips = n_tp // 2
    side = 1
    while side * side < chips:
        side *= 2
    return chips // side, side


def kernel(
    n_ctx, n_tp, tokens_hbm, iw_hbm, gw_hbm, cw_hbm, cb_hbm, pw_hbm, sw_hbm, sb_hbm, dr_hbm, sg_hbm, ow_hbm, cs_hbm,
    mixed, boundary,
    x_buf, iw, gw, ow, pw, sw, cw, cb, sb, sg, dr, cs, acc, gate, pad, tail_in,
    p_send, p_recv, p_more, p_res, step_ref, drive_ref, conv_ref, h_buf, b_chunk, c_chunk, state_out, state_in, sums_out, sums_in, q_buf, y_buf,
    part, sib_part, mine, s1_send, s1_a, s1_b, s2_send, s2_a, s2_b,
    load_sem, ctx_sem, own_send, own_recv, sib_send, sib_recv, tail_sem, red_sem, more_sem, res_sem, state_send, state_recv,
    rs_sib_send, rs_sib_recv, s1_send_sem, s1_a_sem, s1_b_sem, s2_send_sem, s2_a_sem, s2_b_sem,
):
    ny, nx = plane_sides(n_tp)
    chips = ny * nx
    rows, width = tokens_hbm.shape
    half = rows // 2
    s, me = lax.axis_index("ctx"), lax.axis_index("tp")
    core, chip = lax.rem(me, 2), me // 2
    cx, cy = lax.rem(chip, nx), chip // nx

    def chip_at(dx, dy):
        return lax.rem(cy + dy + ny, ny) * nx + lax.rem(cx + dx + nx, nx)

    def tp_at(dx, dy, other=False):
        return chip_at(dx, dy) * 2 + ((1 - core) if other else core)

    def remote(src, dst, send, recv, to, ctx=None):
        return pltpu.make_async_remote_copy(
            src_ref=src, dst_ref=dst, send_sem=send, recv_sem=recv,
            device_id=(s if ctx is None else ctx, to), device_id_type=MESH,
        )

    def await_recv(ref, sem):
        remote(ref, ref, sem, sem, me).wait_recv()

    def await_send(ref, sem):
        remote(ref, ref, sem, sem, me).wait_send()

    barrier = pltpu.get_barrier_semaphore()
    greeted = [(d, 0) for d in range(1, nx)] + [(0, d) for d in range(1, ny)]
    for a, b in greeted:
        pl.semaphore_signal(barrier, inc=1, device_id=(s, tp_at(a, b)), device_id_type=MESH)
    pl.semaphore_signal(barrier, inc=1, device_id=(s, tp_at(0, 0, True)), device_id_type=MESH)
    beside = sorted({1, n_ctx - 1}) if n_ctx > 1 else []

    def signal_ctx(sem, by):
        pl.semaphore_signal(sem, inc=1, device_id=(lax.rem(s + by, n_ctx), me), device_id_type=MESH)

    for by in beside:
        signal_ctx(barrier, by)

    loads = []
    for k, (src, dst) in enumerate(
        [(tokens_hbm, x_buf.at[me]), (iw_hbm, iw), (gw_hbm, gw), (pw_hbm, pw), (sw_hbm, sw), (cw_hbm, cw), (cb_hbm, cb),
         (sb_hbm, sb), (sg_hbm, sg), (dr_hbm, dr), (cs_hbm, cs), (ow_hbm, ow)]
    ):
        loads.append(pltpu.make_async_copy(src, dst, load_sem.at[k]))
        loads[-1].start()

    loads[0].wait()
    pl.semaphore_wait(barrier, len(greeted) + 1 + len(beside))
    rounds = []
    reach = 1
    while 2 * reach < n_ctx:
        rounds.append(reach)
        reach *= 2

    def greet_round(i):
        if i > 0 and i <= len(rounds):
            pl.semaphore_wait(ctx_sem.at[i - 1], 2)
        if i < len(rounds):
            for by in (rounds[i], n_ctx - rounds[i]):
                signal_ctx(ctx_sem.at[i], by)

    greet_round(0)

    top, bottom = pl.ds(0, half), pl.ds(half, half)
    far_first_x = sorted(range(1, nx), key=lambda d: -min(d, nx - d))
    far_first_y = sorted(range(1, ny), key=lambda d: -min(d, ny - d))
    near_x, near_y = far_first_x[::-1], far_first_y[::-1]

    def send_piece(piece, h, dx, dy, rx, ry):
        view = x_buf.at[piece, bottom if h else top]
        remote(view, view, own_send, own_recv.at[rx * ny + ry, h], tp_at(dx, dy)).start()

    def await_piece(rx, ry, h):
        view = x_buf.at[tp_at(-rx, -ry), bottom if h else top]
        await_recv(view, own_recv.at[rx * ny + ry, h])

    def to_sibling(rx, ry):
        view = x_buf.at[tp_at(-rx, -ry)]
        remote(view, view, sib_send, sib_recv.at[rx * ny + ry], tp_at(0, 0, True)).start()

    def from_sibling(rx, ry):
        await_recv(x_buf.at[tp_at(-rx, -ry, True)], sib_recv.at[rx * ny + ry])

    for k in range(max(nx, ny) - 1):
        if k < nx - 1:
            send_piece(me, 0, far_first_x[k], 0, far_first_x[k], 0)
        if k < ny - 1:
            send_piece(me, 1, 0, far_first_y[k], 0, far_first_y[k])
    to_sibling(0, 0)
    for k in range(max(nx, ny) - 1):
        if k < ny - 1:
            send_piece(me, 0, 0, far_first_y[k], 0, far_first_y[k])
        if k < nx - 1:
            send_piece(me, 1, far_first_x[k], 0, far_first_x[k], 0)

    def times(piece, weight):
        first = pl.multiple_of(piece * width, width)
        return dot(x_buf[piece], weight[pl.ds(first, width), :])

    def add_inner(pieces, fresh=False):
        total = sum(times(p, iw) for p in pieces)
        acc[...] = total if fresh else acc[...] + total

    for k in range(max(nx, ny) - 1):
        if k < nx - 1:
            d = near_x[k]
            await_piece(d, 0, 0)
            for e in far_first_y:
                send_piece(tp_at(-d, 0), 0, 0, e, d, e)
        if k < ny - 1:
            d = near_y[k]
            await_piece(0, d, 1)
            for e in far_first_x:
                send_piece(tp_at(0, -d), 1, e, 0, e, d)
    greet_round(1)
    for load in loads[1:]:
        load.wait()
    decay, carried = dr[...], cs[...]
    from_sibling(0, 0)
    add_inner([tp_at(0, 0), tp_at(0, 0, True)], fresh=True)

    waiting = []
    for k in range(max(nx, ny) - 1):
        group = []
        if k < nx - 1:
            group.append((near_x[k], 0))
        if k < ny - 1:
            group.append((0, near_y[k]))
        for rx, ry in group:
            await_piece(rx, ry, 1 if ry == 0 else 0)
            to_sibling(rx, ry)
        for rx, ry in waiting:
            from_sibling(rx, ry)
        add_inner([tp_at(-a, -b) for a, b in group] + [tp_at(-a, -b, True) for a, b in waiting])
        waiting = group
    rest = sorted(
        [(a, b) for a in range(1, nx) for b in range(1, ny)],
        key=lambda r: max(near_x.index(r[0]), near_y.index(r[1])) * 10 + near_x.index(r[0]) + near_y.index(r[1]),
    )
    for k in range(0, len(rest), 3):
        group = rest[k : k + 3]
        for rx, ry in group:
            await_piece(rx, ry, 0)
            await_piece(rx, ry, 1)
            to_sibling(rx, ry)
        for rx, ry in waiting:
            from_sibling(rx, ry)
        add_inner([tp_at(-a, -b) for a, b in group] + [tp_at(-a, -b, True) for a, b in waiting])
        waiting = group
    for rx, ry in waiting:
        from_sibling(rx, ry)
    add_inner([tp_at(-a, -b, True) for a, b in waiting])

    for i in range(2, len(rounds) + 1):
        greet_round(i)

    pad[8:, :] = acc[...].astype(BF16).astype(F32)
    tail = pad.at[pl.ds(rows, 8)]
    first_shard = s == 0

    @pl.when(s < n_ctx - 1)
    def _():
        remote(tail, tail_in, tail_sem.at[0], tail_sem.at[1], me, ctx=lax.rem(s + 1, n_ctx)).start()

    taps = cw.shape[0]
    each = p_send.shape[1]
    across = DT_RANK // 128
    early = across // each
    others = [(a, b, o) for a in range(nx) for b in range(ny) for o in (False, True) if a or b or o]
    others.sort(key=lambda r: -(min(r[0], nx - r[0]) + min(r[1], ny - r[1])))

    def convolve(first, count):
        summed = cb[...] + cw[0:1, :] * pad[9 - taps + first : 9 - taps + first + count, :]
        for k in range(1, taps):
            summed = summed + cw[k : k + 1, :] * pad[9 - taps + first + k : 9 - taps + first + k + count, :]
        low_bits = silu(summed).astype(BF16)
        conv_ref[first : first + count, :] = low_bits.astype(F32)
        return low_bits

    def project(first, conv_low):
        proj = dot_t(conv_low, pw[:DT_RANK, :]).astype(BF16)
        for r in range(first // 16, (first + conv_low.shape[0]) // 16):
            for c in range(across):
                block, at = r * across + c, r * 16 - first
                p_send[block // each, block % each] = proj[at : at + 16, c * 128 : c * 128 + 128]

    def send_block(to):
        remote(p_send.at[to], p_recv.at[me], red_sem.at[0], red_sem.at[1], to).start()

    conv_rest = convolve(16, rows - 16)
    project(16, conv_rest)
    for a, b, other in others:
        to = tp_at(a, b, other)
        pl.when(to >= early)(functools.partial(send_block, to))

    gate[...] = sum(times(p, gw) for p in range(n_tp)).astype(BF16).astype(F32)

    @pl.when(first_shard)
    def _():
        tail_in[...] = jnp.zeros_like(tail_in)

    @pl.when(s > 0)
    def _():
        await_recv(tail_in, tail_sem.at[1])

    pad[0:8, :] = tail_in[...]
    conv_first = convolve(0, 16)
    project(0, conv_first)
    for to in range(early):
        pl.when(me != to)(functools.partial(send_block, to))

    bc = dot_t(pw[DT_RANK:, :], jnp.concatenate([conv_first, conv_rest], axis=0)).astype(BF16)
    p_more[0, me] = bc[:STATE]
    p_more[1, me] = bc[STATE:]
    owners = (0, n_tp // 2)
    for which, owner in enumerate(owners):
        mine_too = p_more.at[which, me]

        @pl.when(me != owner)
        def _():
            remote(mine_too, mine_too, more_sem.at[which, 0], more_sem.at[which, 1], owner).start()

    p_recv[me] = p_send[me]
    await_recv(p_recv.at[pl.ds(0, n_tp - 1)], red_sem.at[1])
    total = p_recv[0].astype(F32)
    for i in range(1, n_tp):
        total = total + p_recv[i].astype(F32)
    p_res[pl.ds(me * each, each)] = total.astype(BF16)
    result = p_res.at[pl.ds(me * each, each)]
    for a, b, other in others:
        remote(result, result, res_sem.at[0], res_sem.at[1], tp_at(a, b, other)).start()
    blocks = n_tp * each
    for which, owner in enumerate(owners):
        place = p_res.at[pl.ds(blocks + which, 1)]

        @pl.when(me == owner)
        def _():
            await_recv(p_more.at[which, pl.ds(0, n_tp - 1)], more_sem.at[which, 1])
            total = p_more[which, 0].astype(F32)
            for i in range(1, n_tp):
                total = total + p_more[which, i].astype(F32)
            p_res[blocks + which] = total.astype(BF16)
            for i in range(1, n_tp):
                remote(place, place, more_sem.at[which, 2], more_sem.at[which, 3], lax.rem(me + i, n_tp)).start()

    await_recv(p_res.at[pl.ds(0, (n_tp - 1) * each)], res_sem.at[1])
    low = jnp.concatenate(
        [jnp.concatenate([p_res[r * across + c] for c in range(across)], axis=1) for r in range(rows // 16)], axis=0
    )
    step = jax.nn.softplus(dot(low, sw[...]) + sb[...])
    step_ref[...] = step
    drive_ref[...] = step * conv_ref[...]
    later = lax.broadcasted_iota(jnp.int32, (rows, rows), 0)
    earlier = lax.broadcasted_iota(jnp.int32, (rows, rows), 1)
    below = (earlier <= later).astype(F32)
    so_far = jnp.dot(below, step, preferred_element_type=F32, precision=lax.Precision.HIGHEST)

    for which, owner in enumerate(owners):

        @pl.when(me != owner)
        def _():
            await_recv(p_res.at[pl.ds(blocks + which, 1)], more_sem.at[which, 3])

    b_t, c_t = p_res[blocks].astype(F32), p_res[blocks + 1].astype(F32)
    run = 16
    for k in range(rows // run):
        turn = (rows - k * run) % rows
        b_chunk[k] = pltpu.roll(b_t, turn, 1) if turn else b_t
        c_chunk[k] = pltpu.roll(c_t, turn, 1) if turn else c_t

    def scan_chunk(k, h):
        first = pl.multiple_of(k * run, run)
        steps, drives, bs = step_ref[pl.ds(first, run), :], drive_ref[pl.ds(first, run), :], b_chunk[k]
        for i in range(run):
            h = jnp.exp(-steps[i : i + 1, :] * decay) * h + drives[i : i + 1, :] * bs[:, i : i + 1]
            h_buf[first + i] = h
        return h

    end = lax.fori_loop(0, rows // run, scan_chunk, jnp.zeros((STATE, width), F32), unroll=True)

    state_out[...] = end.astype(BF16)
    sums_out[...] = so_far[rows - 1 :, :]
    for d in sorted(range(1, n_ctx), key=lambda d: -min(d, n_ctx - d)):

        @pl.when(s + d < n_ctx)
        def _():
            to, slot = lax.rem(s + d, n_ctx), n_ctx - 1 - d
            remote(state_out, state_in.at[slot], state_send.at[d, 0], state_recv.at[d, 0], me, ctx=to).start()
            remote(sums_out, sums_in.at[slot], state_send.at[d, 1], state_recv.at[d, 1], me, ctx=to).start()

    def read_chunk(k, carry):
        first = pl.multiple_of(k * run, run)
        c_now = c_chunk[k]
        lines = []
        for i in range(run):
            lines.append(jnp.sum(h_buf[first + i] * c_now[:, i : i + 1], axis=0, keepdims=True))
        y_buf[pl.ds(first, run), :] = jnp.concatenate(lines, axis=0)
        return carry

    lax.fori_loop(0, rows // run, read_chunk, 0)
    c_rows = jnp.transpose(c_t)
    for n in range(STATE):
        q_buf[n] = c_rows[:, n : n + 1] * jnp.exp(-so_far * decay[n : n + 1, :])
    y_buf[...] = y_buf[...] + sg[...] * conv_ref[...]
    gate[...] = silu(gate[...])

    for d in range(1, n_ctx):

        @pl.when(s >= d)
        def _():
            await_recv(state_in.at[n_ctx - 1 - d], state_recv.at[d, 0])
            await_recv(sums_in.at[n_ctx - 1 - d], state_recv.at[d, 1])

    def enter(i, e):
        return jnp.exp(-decay * sums_in[i]) * e + state_in[i].astype(F32)

    entering = lax.fori_loop(n_ctx - 1 - s, n_ctx - 1, enter, carried)
    boundary[...] = jnp.exp(-decay * sums_out[...]) * entering + end

    readout = y_buf[...]
    for n in range(STATE):
        readout = readout + q_buf[n] * entering[n : n + 1, :]
    gated = (readout * gate[...]).astype(BF16)

    def out_piece(piece):
        first = pl.multiple_of(piece * width, width)
        return dot(gated, ow[:, pl.ds(first, width)])

    def combine(ex, ey):
        r = ex * ny + ey
        await_recv(sib_part.at[r], rs_sib_recv.at[r])
        total = mine[r] + sib_part[r].astype(F32)
        mine[r] = total
        s1_send[r] = total.astype(BF16)
        if ey:
            remote(s1_send.at[r, top], s1_a.at[ey, ex], s1_send_sem, s1_a_sem.at[ey, ex], tp_at(0, ey)).start()
        if ex:
            remote(s1_send.at[r, bottom], s1_b.at[ex, ey], s1_send_sem, s1_b_sem.at[ex, ey], tp_at(ex, 0)).start()

    order = sorted(
        [(a, b) for a in far_first_x for b in far_first_y],
        key=lambda r: (min(far_first_x.index(r[0]), far_first_y.index(r[1])), far_first_x.index(r[0]) + far_first_y.index(r[1])),
    )
    order += [(0, b) for b in far_first_y] + [(a, 0) for a in far_first_x] + [(0, 0)]
    lag = 2
    for k, (ex, ey) in enumerate(order):
        r = ex * ny + ey
        part[r] = out_piece(tp_at(ex, ey, True)).astype(BF16)
        remote(part.at[r], sib_part.at[r], rs_sib_send, rs_sib_recv.at[r], tp_at(0, 0, True)).start()
        mine[r] = out_piece(tp_at(ex, ey))
        if k >= lag:
            combine(*order[k - lag])
    for k in range(max(0, len(order) - lag), len(order)):
        combine(*order[k])

    def second_a(ex):
        total = mine[ex * ny, top, :]
        for e in range(1, ny):
            await_recv(s1_a.at[e, ex], s1_a_sem.at[e, ex])
            total = total + s1_a[e, ex].astype(F32)
        return total

    def second_b(ey):
        total = mine[ey, bottom, :]
        for e in range(1, nx):
            await_recv(s1_b.at[e, ey], s1_b_sem.at[e, ey])
            total = total + s1_b[e, ey].astype(F32)
        return total

    for k in range(max(nx, ny) - 1):
        if k < nx - 1:
            d = far_first_x[k]
            s2_send[0, d] = second_a(d).astype(BF16)
            remote(s2_send.at[0, d], s2_a.at[d], s2_send_sem.at[0, d], s2_a_sem.at[d], tp_at(d, 0)).start()
        if k < ny - 1:
            d = far_first_y[k]
            s2_send[1, d] = second_b(d).astype(BF16)
            remote(s2_send.at[1, d], s2_b.at[d], s2_send_sem.at[1, d], s2_b_sem.at[d], tp_at(0, d)).start()
    upper, lower = second_a(0), second_b(0)
    for d in near_x:
        await_recv(s2_a.at[d], s2_a_sem.at[d])
        upper = upper + s2_a[d].astype(F32)
    mixed[0:half, :] = upper.astype(BF16)
    for d in near_y:
        await_recv(s2_b.at[d], s2_b_sem.at[d])
        lower = lower + s2_b[d].astype(F32)
    mixed[half:, :] = lower.astype(BF16)

    await_send(x_buf.at[pl.ds(0, chips - 1)], own_send)
    await_send(x_buf.at[pl.ds(0, chips)], sib_send)

    @pl.when(s < n_ctx - 1)
    def _():
        await_send(tail, tail_sem.at[0])

    await_send(p_recv.at[pl.ds(0, n_tp - 1)], red_sem.at[0])
    await_send(p_res.at[pl.ds(0, (n_tp - 1) * each)], res_sem.at[0])
    for which, owner in enumerate(owners):

        @pl.when(me != owner)
        def _():
            await_send(p_more.at[which, 0], more_sem.at[which, 0])

        @pl.when(me == owner)
        def _():
            await_send(p_more.at[which, pl.ds(0, n_tp - 1)], more_sem.at[which, 2])

    for d in range(1, n_ctx):

        @pl.when(s + d < n_ctx)
        def _():
            await_send(state_out, state_send.at[d, 0])
            await_send(sums_out, state_send.at[d, 1])

    await_send(sib_part, rs_sib_send)
    for a in range(nx):
        for b in range(ny):
            if b:
                await_send(s1_send.at[0, top], s1_send_sem)
            if a:
                await_send(s1_send.at[0, top], s1_send_sem)
    for d in range(1, nx):
        await_send(s2_send.at[0, d], s2_send_sem.at[0, d])
    for d in range(1, ny):
        await_send(s2_send.at[1, d], s2_send_sem.at[1, d])


def hand_on(a_in, b_in, a_out, b_out):
    a_out[...] = a_in[...]
    b_out[...] = b_in[...]


def on_device(
    n_ctx, n_tp, tokens, inner_weight, gate_weight, conv_weight, conv_bias, proj_weight, step_weight, step_bias, decay_rate,
    skip_gain, out_weight, carried_state,
):
    rows, width = tokens.shape
    depth = inner_weight.shape[0]
    ny, nx = plane_sides(n_tp)
    chips = ny * nx
    half = rows // 2
    each = (rows // 16) * (DT_RANK // 128) // n_tp
    vmem, dma = pltpu.VMEM, pltpu.SemaphoreType.DMA
    args = (
        tokens, inner_weight, gate_weight, conv_weight, conv_bias[None, :], jnp.transpose(proj_weight), step_weight,
        step_bias[None, :], jnp.transpose(decay_rate), skip_gain[None, :], out_weight, jnp.transpose(carried_state),
    )
    held = (inner_weight, gate_weight, out_weight, args[5], step_weight, conv_weight)
    mixed, boundary = pl.pallas_call(
        functools.partial(kernel, n_ctx, n_tp),
        out_shape=(
            jax.ShapeDtypeStruct((rows, width), BF16),
            jax.ShapeDtypeStruct((STATE, width), F32),
        ),
        in_specs=[pl.BlockSpec(memory_space=pl.ANY)] * len(args),
        out_specs=[pl.BlockSpec(memory_space=pltpu.VMEM)] * 2,
        scratch_shapes=[
            vmem((n_tp, rows, width), BF16),
            *[vmem(a.shape, a.dtype) for a in held],
            *[vmem((1, width), F32)] * 3,
            *[vmem((STATE, width), F32)] * 2,
            *[vmem((rows, width), F32)] * 2,
            vmem((rows + 8, width), F32),
            vmem((8, width), F32),
            vmem((n_tp, each, 16, 128), BF16),
            vmem((n_tp, each, 16, 128), BF16),
            vmem((2, n_tp, STATE, 128), BF16),
            vmem((n_tp * each + 2, 16, 128), BF16),
            *[vmem((rows, width), F32)] * 3,
            vmem((rows, STATE, width), F32),
            *[vmem((rows // 16, STATE, rows), F32)] * 2,
            vmem((STATE, width), BF16),
            vmem((n_ctx, STATE, width), BF16),
            vmem((1, width), F32),
            vmem((n_ctx, 1, width), F32),
            vmem((STATE, rows, width), F32),
            vmem((rows, width), F32),
            *[vmem((chips, rows, width), BF16)] * 2,
            vmem((chips, rows, width), F32),
            vmem((chips, rows, width), BF16),
            vmem((ny, nx, half, width), BF16),
            vmem((nx, ny, half, width), BF16),
            vmem((2, max(nx, ny), half, width), BF16),
            vmem((nx, half, width), BF16),
            vmem((ny, half, width), BF16),
            dma((len(args),)),
            pltpu.SemaphoreType.REGULAR((4,)),
            dma,
            dma((chips, 2)),
            dma,
            dma((chips,)),
            dma((2,)),
            dma((2,)),
            dma((2, 4)),
            dma((2,)),
            dma((n_ctx, 2)),
            dma((n_ctx, 2)),
            dma,
            dma((chips,)),
            dma,
            dma((ny, nx)),
            dma((nx, ny)),
            dma((2, max(nx, ny))),
            dma((nx,)),
            dma((ny,)),
        ],
        compiler_params=pltpu.CompilerParams(collective_id=0, has_side_effects=True, vmem_limit_bytes=56 << 20),
        cost_estimate=pl.CostEstimate(
            flops=2 * rows * width * (3 * depth + 544 + 512), bytes_accessed=3 * depth * width * 2, transcendentals=0
        ),
        name="layer",
    )(*args)
    mixed, boundary = pl.pallas_call(
        hand_on,
        out_shape=(
            jax.ShapeDtypeStruct((rows, width), BF16),
            jax.ShapeDtypeStruct((STATE, width), F32),
        ),
        in_specs=[pl.BlockSpec(memory_space=pltpu.VMEM)] * 2,
        out_specs=[pl.BlockSpec(memory_space=pltpu.VMEM)] * 2,
        cost_estimate=pl.CostEstimate(flops=0, bytes_accessed=4 * rows * width, transcendentals=0),
        name="results",
    )(mixed, boundary)
    return mixed, jnp.transpose(boundary)[None]


def solution(mesh):
    in_specs = (
        P("ctx", "tp"), P(None, "tp"), P(None, "tp"), P(None, "tp"), P("tp"), P("tp", None), P(None, "tp"), P("tp"),
        P("tp", None), P("tp"), P("tp", None), P("tp", None),
    )
    out_specs = (P("ctx", "tp"), P("ctx", "tp", None))
    body = functools.partial(on_device, mesh.shape["ctx"], mesh.shape["tp"])
    return jax.shard_map(body, mesh=mesh, in_specs=in_specs, out_specs=out_specs, check_vma=False)
```
